128 devices in a mesh: wide: 64 (over z, x, y), narrow: 2 (over core).
Axes of the slice: x: 4, y: 4, z: 4, core: 2. Of those that a mesh axis runs over, the one named last changes fastest.
Arguments:
- patches: bfloat16 [32768, 1152], P('wide'), may hold values from -6 to 6
- vision_gain: float32 [1152], replicated, may hold values from 0.1 to 1.9
- vision_up: bfloat16 [1152, 2304], P(None, 'narrow'), may hold values from -0.1875 to 0.1875
- vision_down: bfloat16 [2304, 1152], P('narrow'), may hold values from -0.125 to 0.125
- merger: bfloat16 [4608, 2048], P(None, 'narrow'), may hold values from -0.09375 to 0.09375
- visual_spots: int32 [8192], P('wide'), may hold values from 0 to 127, as said below
- text_embed: bfloat16 [16384, 2048], P(('wide', 'narrow')), may hold values from -6 to 6
- queries: bfloat16 [16384, 4096], P(('wide', 'narrow')), may hold values from -66 to 66
- attention_gain: float32 [2048], replicated, may hold values from 0.1 to 1.9
- key_proj: bfloat16 [2048, 256], replicated, may hold values from -0.125 to 0.125
- value_proj: bfloat16 [2048, 256], replicated, may hold values from -0.125 to 0.125
- prompt_lengths: int32 [64], P('wide'), may hold values from 32 to 256
- expert_gain: float32 [2048], replicated, may hold values from 0.1 to 1.9
- routes: int32 [16384, 8], P(('wide', 'narrow')), may hold values from 0 to 63, all different within a row; in each aligned block of 128 rows (0 to 127, 128 to 255, ...) at most 24 rows name the same one
- route_weight: float32 [16384, 8], P(('wide', 'narrow')), may hold values from 0.05 to 1
- gate_weight: bfloat16 [64, 2048, 768], P('wide', None, 'narrow'), may hold values from -0.125 to 0.125
- up_weight: bfloat16 [64, 2048, 768], P('wide', None, 'narrow'), may hold values from -0.125 to 0.125
- down_weight: bfloat16 [64, 768, 2048], P('wide', 'narrow'), may hold values from -0.21875 to 0.21875
Outputs:
- attended: bfloat16 [16384, 4096], P(('wide', 'narrow'))
- expert_mix: bfloat16 [16384, 2048], P(('wide', 'narrow'))
The draws below stay inside these ranges and needn't reach their ends.
Inputs may be any that keep to these rules, and one draw needn't show every extreme that they name: `visual_spots`: merged token i of the 128 of a wide index goes to device i // (128 // the number of devices) in the order wide index, narrow index; the positions that reach one device are distinct. `routes`: among the 128 rows of one device no expert is named more than 24 times.
All inputs are finite; a program needn't handle non-finite values.
Results may differ from the reference program's by a relative error of at most 0.02.
Values may be sent and summed in bfloat16 or wider, within the bound.
A program may use at most 192 MiB of HBM per device.

```python
import math
import jax
import jax.numpy as jnp
import numpy as np
from jax import lax

DV = 1152
FV = 2304
MERGE = 4
D = 2048
HQ = 32
KVH = 2
HD = 128
FE = 768
TOPK = 8
TOK_DEV = 128
V_DEV = 128
TOKENS = 16384
PATCHES = 32768
VIS = 8192
EXPERTS = 64
CAP = 24
N_WIDE = 64
N_NARROW = 2


def draw_visual_spots(key, part):
    key = jax.random.fold_in(key, 5)
    device_total = N_WIDE * N_NARROW
    key_table = jax.random.split(key, device_total)

    def one_order(single_key):
        return jax.random.permutation(single_key, TOK_DEV)
    orders = jax.vmap(one_order)(key_table)
    per_dest = V_DEV // device_total
    chosen = orders[:, :N_WIDE * per_dest].reshape(device_total, N_WIDE, per_dest)
    return jnp.transpose(chosen, (1, 0, 2)).reshape(-1).astype(jnp.int32)


def draw_queries(key, part):
    key = jax.random.fold_in(key, 11)
    first_key = jax.random.fold_in(key, 0)
    return jnp.clip(jax.random.normal(first_key, (TOKENS, HQ * HD)), -6.0, 6.0).astype(jnp.bfloat16)


def touch_ends(drawn, rng, smallest, high):
    longest = drawn.shape.index(max(drawn.shape))
    spots = []
    for shift in (0, 1):
        where = [jax.random.randint(jax.random.fold_in(rng, axis), (), 0, length) for axis, length in enumerate(drawn.shape)]
        where[longest] = (where[longest] + shift) % drawn.shape[longest]
        spots.append(tuple(where))
    return drawn.at[spots[0]].set(smallest).at[spots[1]].set(high)


def shard_levels(own_key, dims, shards, least, top_value):
    loudness = 1.0
    for position, shards_of in shards:
        heights = jax.random.uniform(jax.random.fold_in(jax.random.fold_in(own_key, 6), position), (shards_of,), jnp.float32, least / len(shards), top_value / len(shards))
        loudness = loudness * jnp.repeat(jnp.exp(heights), dims[position] // shards_of).reshape((-1,) + (1,) * (len(dims) - 1 - position))
    return loudness


def assign_block(key, own, number, rows, amount, top, reach, lean):
    sequence = jax.random.permutation(key, amount)
    crowded, common = portions_of(amount, rows * top, reach, lean, True), portions_of(amount, rows * top, reach, lean, False)
    places = jnp.arange(amount)

    def named(lengths, rotation):
        used = int((lengths > 0).sum())
        fixed = max(1, used // 4)
        shifted = fixed + (places - fixed + rotation * (used - fixed)) % max(1, amount - fixed)
        return jnp.zeros((amount,), jnp.int32).at[sequence[jnp.where(places < fixed, places, shifted)]].set(jnp.asarray(lengths, jnp.int32))

    lengths = jnp.where(number % 4 == 0, named(crowded, number // 4), named(common, number - number // 4 - 1))
    mixed = jax.random.permutation(jax.random.fold_in(own, 3), amount)
    source_of, sink = mixed[0:amount // 2 * 2:2], mixed[1:amount // 2 * 2:2]
    room = jnp.minimum(lengths[source_of] - 1, reach - lengths[sink]) // 2
    room = jnp.where((source_of == sequence[0]) | (sink == sequence[0]) | (lengths[sink] == 0), 0, jnp.maximum(room, 0))
    shifted = jax.random.randint(jax.random.fold_in(own, 4), (amount // 2,), 0, 1 << 20) % (room + 1)
    lengths = lengths.at[source_of].add(-shifted).at[sink].add(shifted)
    items = jnp.searchsorted(jnp.cumsum(lengths), jnp.arange(rows * top), side="right").astype(jnp.int32)
    grid = items.reshape(top, rows).T
    grid = grid[jax.random.permutation(jax.random.fold_in(own, 1), rows)]
    rotation = jax.random.randint(jax.random.fold_in(own, 2), (rows, 1), 0, top)
    return jnp.take_along_axis(grid, (jnp.arange(top)[None, :] + rotation) % top, axis=1)


def portions_of(number_of, total, reach, slope, full):
    weights = [(1 << 20) // math.isqrt(rank ** slope) + 1 for rank in range(1, number_of + 1)]
    largest = reach if full else min(reach, max(-(-total // number_of), total * weights[0] // sum(weights)))
    least = 1 if total - largest >= number_of - 1 else 0
    given, rest = [largest] + [least] * (number_of - 1), total - largest - least * (number_of - 1)
    while rest > 0:
        candidates = [i for i in range(1, number_of) if given[i] < largest] or [i for i in range(1, number_of) if given[i] < reach]
        mass, remaining = sum([weights[i] for i in candidates]), rest
        for i in candidates:
            extra = min(reach - given[i], max(1, remaining * weights[i] // mass), rest)
            given[i] = given[i] + extra
            rest = rest - extra
    return np.array(given)


def scatter_about(stream_key, shape, width, bound, pieces=(), kind=jnp.bfloat16):
    factor_of = shard_levels(stream_key, shape, pieces, -0.22, 0.18) if pieces else 1.0
    values = jax.random.normal(stream_key, shape, jnp.float32) * width * factor_of
    return jnp.minimum(jnp.maximum(values, -bound), bound).astype(kind)


def setup_inputs(seed: int = 0) -> dict:
    keys = jax.random.split(jax.random.key(seed), 19)
    patches = scatter_about(keys[0], (PATCHES, DV), 1.0, 6.0, ((0, 64),))
    vision_gain = jnp.clip(1.0 + 0.18 * jax.random.normal(keys[1], (DV,), jnp.float32), 0.1, 1.9)
    vision_up = scatter_about(keys[2], (DV, FV), DV ** -0.5, 0.1875, ((1, 2),))
    vision_down = scatter_about(keys[3], (FV, DV), FV ** -0.5, 0.125, ((0, 2),))
    merger = scatter_about(keys[4], (MERGE * DV, D), (MERGE * DV) ** -0.5, 0.09375, ((1, 2),))
    visual_spots = draw_visual_spots(jax.random.fold_in(keys[18], 71), 0)
    text_embed = scatter_about(keys[6], (TOKENS, D), 1.0, 6.0, ((0, 128),))
    queries = draw_queries(jax.random.fold_in(keys[18], 71), 0)
    attention_gain = jnp.clip(1.0 + 0.18 * jax.random.normal(keys[8], (D,), jnp.float32), 0.1, 1.9)
    key_proj = scatter_about(keys[9], (D, KVH * HD), D ** -0.5, 0.125)
    value_proj = scatter_about(keys[10], (D, KVH * HD), D ** -0.5, 0.125)
    prompt_lengths = touch_ends(jax.random.randint(keys[11], (N_WIDE,), TOK_DEV // 4, TOK_DEV * N_NARROW + 1), jax.random.fold_in(keys[11], 1), TOK_DEV // 4, TOK_DEV * N_NARROW).astype(jnp.int32)
    expert_gain = jnp.clip(1.0 + 0.18 * jax.random.normal(keys[12], (D,), jnp.float32), 0.1, 1.9)
    routes_keys = jax.random.split(jax.random.fold_in(keys[13], 1), TOKENS // TOK_DEV)
    routes_turns = jax.random.permutation(jax.random.fold_in(keys[13], 3), TOKENS // TOK_DEV)
    routes = jax.vmap(lambda own, number: assign_block(jax.random.fold_in(keys[13], 2), own, number, TOK_DEV, EXPERTS, TOPK, CAP, 2))(routes_keys, routes_turns).reshape((TOKENS, TOPK))
    route_weight = jnp.clip(jnp.exp(math.log(1.0) - 2.9957323 * jax.random.uniform(keys[14], (TOKENS, TOPK), jnp.float32) ** shard_levels(keys[14], (TOKENS, TOPK), ((0, 128),), -0.2, 0.2)), 0.05, 1.0)
    gate_weight = scatter_about(keys[15], (EXPERTS, D, FE), D ** -0.5, 0.125, ((0, 64), (2, 2)))
    up_weight = scatter_about(keys[16], (EXPERTS, D, FE), D ** -0.5, 0.125, ((0, 64), (2, 2)))
    down_weight = scatter_about(keys[17], (EXPERTS, FE, D), FE ** -0.5, 0.21875, ((0, 64), (1, 2)))
    return dict(patches=patches, vision_gain=vision_gain, vision_up=vision_up, vision_down=vision_down, merger=merger, visual_spots=visual_spots, text_embed=text_embed, queries=queries, attention_gain=attention_gain, key_proj=key_proj, value_proj=value_proj, prompt_lengths=prompt_lengths, expert_gain=expert_gain, routes=routes, route_weight=route_weight, gate_weight=gate_weight, up_weight=up_weight, down_weight=down_weight)


EPSILON = 1e-06

def layer_norm(values, gain):
    mean_value = lax.optimization_barrier(jnp.mean(values, axis=-1, keepdims=True))
    centered = values - mean_value
    variance = lax.optimization_barrier(jnp.mean(centered * centered, axis=-1, keepdims=True))
    return centered * lax.rsqrt(variance + EPSILON) * gain

def rms_scale(values):
    return lax.rsqrt(lax.optimization_barrier(jnp.mean(values * values, axis=-1, keepdims=True)) + EPSILON)

def expert_apply(rows_in, gate_part, up_part, down_part):
    gate_act = jnp.dot(rows_in, gate_part, preferred_element_type=jnp.float32)
    up_act = jnp.dot(rows_in, up_part, preferred_element_type=jnp.float32)
    active = (jax.nn.silu(gate_act) * up_act).astype(jnp.bfloat16)
    return jnp.dot(active, down_part, preferred_element_type=jnp.float32)

def attend_block(query_rows, key_rows, value_rows, valid_limit):
    row_count = query_rows.shape[0]
    group_size = HQ // KVH
    query_heads = query_rows.astype(jnp.float32).reshape(row_count, KVH, group_size, HD)
    key_heads = key_rows.astype(jnp.float32).reshape(row_count, KVH, HD)
    value_heads = value_rows.astype(jnp.float32).reshape(row_count, KVH, HD)
    scores = jnp.einsum('tkgd,skd->kgts', query_heads, key_heads) * HD ** (-0.5)
    query_pos = jnp.arange(row_count, dtype=jnp.int32)
    allowed = (query_pos[None, :] <= query_pos[:, None]) & (query_pos[None, :] < valid_limit)
    scores = jnp.where(allowed, scores, -1e+30)
    row_max = lax.optimization_barrier(jnp.max(scores, axis=-1, keepdims=True))
    weights = jnp.exp(scores - row_max)
    denominator = lax.optimization_barrier(jnp.sum(weights, axis=-1))
    rounded = lax.optimization_barrier(weights.astype(jnp.bfloat16)).astype(jnp.float32)
    mixed_out = jnp.einsum('kgts,skd->tkgd', rounded, value_heads)
    mixed_out = mixed_out / jnp.transpose(denominator, (2, 0, 1))[..., None]
    return mixed_out.reshape(row_count, HQ * HD).astype(jnp.bfloat16)

def reference(patches, vision_gain, vision_up, vision_down, merger, visual_spots, text_embed, queries, attention_gain, key_proj, value_proj, prompt_lengths, expert_gain, routes, route_weight, gate_weight, up_weight, down_weight):
    patch_rows = patches.astype(jnp.float32)
    normed = layer_norm(patch_rows, vision_gain).astype(jnp.bfloat16)
    inner_act = jax.nn.gelu(jnp.dot(normed, vision_up, preferred_element_type=jnp.float32), approximate=True).astype(jnp.bfloat16)
    vision_out = (patch_rows + jnp.dot(inner_act, vision_down, preferred_element_type=jnp.float32)).astype(jnp.bfloat16)
    merged = vision_out.reshape(VIS, MERGE * DV)
    visual = jnp.dot(merged, merger, preferred_element_type=jnp.float32).astype(jnp.bfloat16)
    within = jnp.arange(VIS, dtype=jnp.int32) % V_DEV
    owner_dev = within // (V_DEV // (N_WIDE * N_NARROW))
    global_pos = (owner_dev * TOK_DEV + visual_spots).astype(jnp.int32)
    hidden = text_embed.at[global_pos].set(visual)
    hidden_f = hidden.astype(jnp.float32)
    scale_rows = rms_scale(hidden_f)
    attn_in = (hidden_f * scale_rows * attention_gain).astype(jnp.bfloat16)
    key_list = jnp.dot(attn_in, key_proj, preferred_element_type=jnp.float32).astype(jnp.bfloat16)
    value_list = jnp.dot(attn_in, value_proj, preferred_element_type=jnp.float32).astype(jnp.bfloat16)
    prompt_len = TOK_DEV * N_NARROW

    def one_prompt(packed):
        query_rows, key_rows, value_rows, valid_limit = packed
        return attend_block(query_rows, key_rows, value_rows, valid_limit)
    attended = lax.map(one_prompt, (queries.reshape(N_WIDE, prompt_len, HQ * HD), key_list.reshape(N_WIDE, prompt_len, KVH * HD), value_list.reshape(N_WIDE, prompt_len, KVH * HD), prompt_lengths))
    attended = attended.reshape(TOKENS, HQ * HD)
    moe_in = (hidden_f * scale_rows * expert_gain).astype(jnp.bfloat16)
    rows_cap = CAP * N_WIDE * N_NARROW
    flat_route = routes.reshape(-1)
    flat_weight = route_weight.reshape(-1)

    def one_expert(running_sum, expert_id):
        chosen_mask = flat_route == expert_id
        picked_ids = jnp.nonzero(chosen_mask, size=rows_cap, fill_value=0)[0].astype(jnp.int32)
        live_mask = jnp.arange(rows_cap, dtype=jnp.int32) < jnp.sum(chosen_mask.astype(jnp.int32))
        token_ids = picked_ids // TOPK
        rows_in = moe_in[token_ids]
        gate_part = lax.dynamic_index_in_dim(gate_weight, expert_id, 0, keepdims=False)
        up_part = lax.dynamic_index_in_dim(up_weight, expert_id, 0, keepdims=False)
        down_part = lax.dynamic_index_in_dim(down_weight, expert_id, 0, keepdims=False)
        produced = expert_apply(rows_in, gate_part, up_part, down_part)
        produced = lax.optimization_barrier(produced.astype(jnp.bfloat16)).astype(jnp.float32)
        factor = jnp.where(live_mask, flat_weight[picked_ids], jnp.zeros_like(flat_weight[picked_ids]))
        running_sum = running_sum.at[token_ids].add(produced * factor[:, None])
        return (running_sum, None)
    running_sum, unused = lax.scan(one_expert, jnp.zeros((TOKENS, D), jnp.float32), jnp.arange(EXPERTS, dtype=jnp.int32))
    return (attended, running_sum.astype(jnp.bfloat16))
```

```python
import functools

import jax
import jax.numpy as jnp
from jax import lax
from jax.experimental import pallas as pl
from jax.experimental.pallas import tpu as pltpu
from jax.sharding import PartitionSpec as P

MERGE = 4
HQ = 32
KVH = 2
HD = 128
D = 2048
FE = 768
HALF = FE // 2
CAP = 24
TOK = 128
LINE = 4
ROWS = LINE * CAP
EPSILON = 1e-06
MESH = pl.DeviceIdType.MESH
BF16 = jnp.bfloat16
F32 = jnp.float32

SLICES = ((0, 640), (640, 640), (1280, 768))
ORDERS = ((0, 1, 2), (1, 2, 0), (2, 0, 1))
FAR_FIRST = (2, 1, 3)


def wide_of(place):
    return place[0] * 16 + place[1] * 4 + place[2]


def shifted(place, axis, step):
    moved = list(place)
    moved[axis] = lax.rem(place[axis] + step + 4, 4)
    return tuple(moved)


def source_index(order, ka, kb, kc):
    offset = [0, 0, 0]
    offset[order[0]], offset[order[1]], offset[order[2]] = ka, kb, kc
    return offset[0] * 16 + offset[1] * 4 + offset[2]


def lane_iota(shape, dim):
    return lax.broadcasted_iota(jnp.int32, shape, dim)


def expert_kernel(
    hidden_ref, again_ref, egain_ref, routes_ref, rweight_ref, length_ref,
    queries_hbm, kproj_hbm, vproj_hbm, gate_hbm, up_hbm, down_hbm,
    attended_ref, mix_ref,
    gu, dn, acc, part, queries, kproj, vproj, kv, tables,
    g0, g1, g2, tx0, tx1, tx2, mid0, mid1, mid2, rx0, rx1, rx2, fin0, fin1, fin2,
    local_sem, wsend, wrecv, kvsend, kvrecv, tsend, trecv,
    s1send, s1recv, s2send, s2recv, s3send, s3recv,
    r1send, r1recv, r2send, r2recv, r3send, r3recv, free_sem,
):
    gs, txs, mids, rxs, fins = (
        (g0, g1, g2), (tx0, tx1, tx2), (mid0, mid1, mid2), (rx0, rx1, rx2), (fin0, fin1, fin2)
    )
    wide = lax.axis_index("wide")
    narrow = lax.axis_index("narrow")
    place = (wide // 16, lax.rem(wide // 4, 4), lax.rem(wide, 4))

    def peer(axis, step):
        return (wide_of(shifted(place, axis, step)), narrow)

    partner = (wide, 1 - narrow)
    barrier = pltpu.get_barrier_semaphore()
    for axis in range(3):
        for step in (1, 2, 3):
            pl.semaphore_signal(barrier, inc=1, device_id=peer(axis, step), device_id_type=MESH)
    pl.semaphore_signal(barrier, inc=1, device_id=partner, device_id_type=MESH)

    def remote(src, dst, send, recv, device):
        return pltpu.make_async_remote_copy(
            src_ref=src, dst_ref=dst, send_sem=send, recv_sem=recv, device_id=device,
            device_id_type=MESH,
        )

    loads = [
        pltpu.make_async_copy(kproj_hbm, kproj, local_sem.at[0]),
        pltpu.make_async_copy(vproj_hbm, vproj, local_sem.at[1]),
        pltpu.make_async_copy(queries_hbm, queries, local_sem.at[2]),
        pltpu.make_async_copy(gate_hbm.at[0], gu.at[:, 0:HALF], local_sem.at[3]),
        pltpu.make_async_copy(up_hbm.at[0], gu.at[:, FE:FE + HALF], local_sem.at[4]),
        pltpu.make_async_copy(down_hbm.at[0], dn.at[0:HALF, :], local_sem.at[5]),
    ]
    for load in loads:
        load.start()

    expert_iota = lane_iota((64, TOK), 0)
    member = jnp.zeros((64, TOK), F32)
    weight = jnp.zeros((64, TOK), F32)
    for k in range(8):
        hit = routes_ref[k:k + 1, :] == expert_iota
        member = member + jnp.where(hit, 1.0, 0.0)
        weight = weight + jnp.where(hit, rweight_ref[k:k + 1, :], 0.0)
    before = (lane_iota((TOK, TOK), 0) < lane_iota((TOK, TOK), 1)).astype(F32).astype(BF16)
    rank = jnp.dot(member.astype(BF16), before, preferred_element_type=F32)
    tables[0, 0] = jnp.where(member > 0.5, rank, -1.0)
    tables[0, 1] = weight

    hidden = hidden_ref[...].astype(F32)
    scale = lax.rsqrt(jnp.mean(hidden * hidden, axis=-1, keepdims=True) + EPSILON)
    scaled = hidden * scale
    moe_in = (scaled * egain_ref[...]).astype(BF16)
    attn_in = (scaled * again_ref[...]).astype(BF16)
    for s, (start, width) in enumerate(SLICES):
        gs[s][0] = moe_in[:, start:start + width]

    pl.semaphore_wait(barrier, 10)

    table_copies = []
    hop1 = {}
    for axis in range(3):
        for step in (1, 2, 3):
            slot = 1 + axis * 3 + step - 1
            copy = remote(
                tables.at[0], tables.at[slot], tsend.at[slot], trecv.at[slot], peer(axis, step)
            )
            copy.start()
            table_copies.append(copy)
    for s in range(3):
        for k in FAR_FIRST:
            copy = remote(
                gs[s].at[0], gs[s].at[k], s1send.at[s, k], s1recv.at[s, k], peer(ORDERS[s][0], k)
            )
            copy.start()
            hop1[s, k] = copy

    loads[0].wait()
    loads[1].wait()
    own_keys = jnp.dot(attn_in, kproj[...], preferred_element_type=F32).astype(BF16)
    own_values = jnp.dot(attn_in, vproj[...], preferred_element_type=F32).astype(BF16)
    kv[narrow, :, 0:KVH * HD] = own_keys
    kv[narrow, :, KVH * HD:] = own_values
    kv_copy = remote(kv.at[narrow], kv.at[narrow], kvsend, kvrecv, partner)
    kv_copy.start()
    weight_copies = [
        remote(gate_hbm.at[0], gu.at[:, HALF:FE], wsend.at[0], wrecv.at[0], partner),
        remote(up_hbm.at[0], gu.at[:, FE + HALF:], wsend.at[1], wrecv.at[1], partner),
        remote(down_hbm.at[0], dn.at[HALF:, :], wsend.at[2], wrecv.at[2], partner),
    ]
    for copy in weight_copies:
        copy.start()

    slot_iota = lane_iota((ROWS, LINE * TOK), 0).astype(F32)

    def slot_blocks(s, kb, weighted):
        axis_a, axis_b, axis_c = ORDERS[s]
        blocks = []
        for kc in range(4):
            expert = wide_of(shifted(shifted(place, axis_b, kb), axis_c, kc))
            rows = []
            weights = []
            for ka in range(4):
                slot = 0 if ka == 0 else 1 + axis_a * 3 + ka - 1
                row = tables[slot, 0, pl.ds(expert, 1), :]
                rows.append(jnp.where(row >= 0.0, row + float(CAP * ka), -1.0))
                if weighted:
                    weights.append(tables[slot, 1, pl.ds(expert, 1), :])
            hit = slot_iota == jnp.concatenate(rows, axis=1)
            if weighted:
                value = jnp.where(hit, jnp.concatenate(weights, axis=1), 0.0)
            else:
                value = jnp.where(hit, 1.0, 0.0)
            blocks.append(value.astype(BF16))
        return jnp.concatenate(blocks, axis=0)

    for copy in table_copies:
        copy.wait_recv()

    hop2 = {}
    for s, (start, width) in enumerate(SLICES):
        for k in (1, 2, 3):
            hop1[s, k].wait_recv()
    for kb in (2, 1, 3, 0):
        for s, (start, width) in enumerate(SLICES):
            tokens = gs[s][...].reshape(LINE * TOK, width)
            rows = jnp.dot(slot_blocks(s, kb, False), tokens, preferred_element_type=F32)
            rows = rows.astype(BF16).reshape(4, ROWS, width)
            if kb == 0:
                mids[s][0] = rows
            else:
                txs[s][kb] = rows
                copy = remote(
                    txs[s].at[kb], mids[s].at[kb], s2send.at[s, kb], s2recv.at[s, kb],
                    peer(ORDERS[s][1], kb),
                )
                copy.start()
                hop2[s, kb] = copy

    hop3 = {}

    def forward(kb):
        for s in range(3):
            if kb:
                hop2[s, kb].wait_recv()
            for kc in FAR_FIRST:
                copy = remote(
                    mids[s].at[kb, kc], rxs[s].at[kc, kb], s3send.at[s, kc, kb],
                    s3recv.at[s, kc, kb], peer(ORDERS[s][2], kc),
                )
                copy.start()
                hop3[s, kc, kb] = copy

    forward(0)

    kv_copy.wait_recv()
    loads[2].wait()
    row_pos = lane_iota((TOK, 2 * TOK), 0) + narrow * TOK
    key_pos = lane_iota((TOK, 2 * TOK), 1)
    limit = jnp.minimum(row_pos, length_ref[0] - 1)
    allowed = key_pos <= limit

    def attend(head, group):
        columns = pl.ds(pl.multiple_of(head * HD, HD), HD)
        keys = kv[:, :, group * HD:(group + 1) * HD].reshape(2 * TOK, HD)
        values = kv[:, :, (KVH + group) * HD:(KVH + group + 1) * HD].reshape(2 * TOK, HD)
        scores = lax.dot_general(
            queries[:, columns], keys, (((1,), (1,)), ((), ())), preferred_element_type=F32
        ) * HD ** (-0.5)
        scores = jnp.where(allowed, scores, -1e30)
        row_max = jnp.max(scores, axis=-1, keepdims=True)
        weights = jnp.exp(scores - row_max)
        total = jnp.sum(weights, axis=-1, keepdims=True)
        mixed = jnp.dot(weights.astype(BF16), values, preferred_element_type=F32)
        attended_ref[:, columns] = (mixed / total).astype(BF16)

    group_size = HQ // KVH

    def attend_heads(first, count, group):
        def body(i, carry):
            for j in range(4):
                attend(first + i * 4 + j, group)
            return carry
        lax.fori_loop(0, count // 4, body, 0)

    attend_heads(0, 16, 0)
    forward(1)
    forward(3)
    attend_heads(16, 16, 1)
    for copy in hop2.values():
        copy.wait_send()
    forward(2)

    for load in loads[3:]:
        load.wait()
    for copy in weight_copies:
        copy.wait_recv()

    written = set()

    def project(s, kc):
        start, width = SLICES[s]
        if kc:
            for kb in range(4):
                hop3[s, kc, kb].wait_recv()
            rows = rxs[s][kc].reshape(4 * ROWS, width)
        else:
            rows = mids[s][:, 0].reshape(4 * ROWS, width)
        for n in range(2):
            out = jnp.dot(
                rows, gu[start:start + width, n * FE:(n + 1) * FE], preferred_element_type=F32
            ).reshape(4, 4, CAP, FE)
            for kb in range(4):
                for ka in range(4):
                    index = source_index(ORDERS[s], ka, kb, kc)
                    if (n, index) in written:
                        acc[index, :, n * FE:(n + 1) * FE] += out[kb, ka]
                    else:
                        written.add((n, index))
                        acc[index, :, n * FE:(n + 1) * FE] = out[kb, ka]

    for kc in (0, 1, 3, 2):
        for s in range(3):
            project(s, kc)

    def activate(i, carry):
        gate = acc[i, :, 0:FE]
        up = acc[i, :, FE:]
        acc[i, :, 0:FE] = gate * (1.0 / (1.0 + jnp.exp(-gate))) * up
        return carry

    lax.fori_loop(0, 64, activate, 0)

    for copy in hop3.values():
        copy.wait_send()
    for s in range(3):
        for kb in (1, 2, 3):
            pl.semaphore_signal(
                free_sem.at[s, kb], inc=1, device_id=peer(ORDERS[s][1], kb), device_id_type=MESH
            )

    back1 = {}
    for kc in (2, 1, 3, 0):
        for s, (start, width) in enumerate(SLICES):
            pieces = [
                acc[source_index(ORDERS[s], ka, kb, kc), :, 0:FE]
                for kb in range(4) for ka in range(4)
            ]
            active = jnp.concatenate(pieces, axis=0).astype(BF16)
            out = jnp.dot(active, dn[:, start:start + width], preferred_element_type=F32)
            out = out.astype(BF16).reshape(4, ROWS, width)
            if kc == 0:
                txs[s][:, 0] = out
            else:
                rxs[s][kc] = out
                for kb in (2, 1, 3, 0):
                    copy = remote(
                        rxs[s].at[kc, kb], txs[s].at[kb, kc], r1send.at[s, kc, kb],
                        r1recv.at[s, kc, kb], peer(ORDERS[s][2], -kc),
                    )
                    copy.start()
                    back1[s, kc, kb] = copy

    back2 = {}
    for kb in (2, 1, 3, 0):
        for s in range(3):
            for kc in (2, 1, 3):
                back1[s, kc, kb].wait_recv()
            if kb:
                pl.semaphore_wait(free_sem.at[s, kb], 1)
                copy = remote(
                    txs[s].at[kb], mids[s].at[kb], r2send.at[s, kb], r2recv.at[s, kb],
                    peer(ORDERS[s][1], -kb),
                )
                copy.start()
                back2[s, kb] = copy

    for kb in (0, 1, 3, 2):
        for s, (start, width) in enumerate(SLICES):
            if kb:
                back2[s, kb].wait_recv()
                rows = mids[s][kb].reshape(4 * ROWS, width)
            else:
                rows = txs[s][0].reshape(4 * ROWS, width)
            total = lax.dot_general(
                slot_blocks(s, kb, True), rows, (((0,), (0,)), ((), ())),
                preferred_element_type=F32,
            )
            if kb:
                part[:, start:start + width] += total
            else:
                part[:, start:start + width] = total

    back3 = {}
    for s, (start, width) in enumerate(SLICES):
        for k in FAR_FIRST:
            gs[s][k] = part[k * TOK:(k + 1) * TOK, start:start + width].astype(BF16)
            copy = remote(
                gs[s].at[k], fins[s].at[k], r3send.at[s, k], r3recv.at[s, k],
                peer(ORDERS[s][0], -k),
            )
            copy.start()
            back3[s, k] = copy
    for s, (start, width) in enumerate(SLICES):
        total = part[0:TOK, start:start + width]
        for k in (1, 3, 2):
            back3[s, k].wait_recv()
            total = total + fins[s][k].astype(F32)
        mix_ref[:, start:start + width] = total.astype(BF16)

    kv_copy.wait_send()
    for copies in (table_copies, weight_copies, hop1.values(), back1.values(), back2.values(),
                   back3.values()):
        for copy in copies:
            copy.wait_send()


def experts_and_attention(
    hidden, again, egain, routes, rweight, lengths, queries, kproj, vproj, gate, up, down
):
    vmem = pl.BlockSpec(memory_space=pltpu.VMEM)
    smem = pl.BlockSpec(memory_space=pltpu.SMEM)
    hbm = pl.BlockSpec(memory_space=pl.ANY)
    dma = pltpu.SemaphoreType.DMA
    widths = [width for _, width in SLICES]
    scratch = [
        pltpu.VMEM((D, 2 * FE), BF16),
        pltpu.VMEM((FE, D), BF16),
        pltpu.VMEM((64, CAP, 2 * FE), F32),
        pltpu.VMEM((LINE * TOK, D), F32),
        pltpu.VMEM((TOK, HQ * HD), BF16),
        pltpu.VMEM((D, KVH * HD), BF16),
        pltpu.VMEM((D, KVH * HD), BF16),
        pltpu.VMEM((2, TOK, 2 * KVH * HD), BF16),
        pltpu.VMEM((10, 2, 64, TOK), F32),
    ]
    scratch += [pltpu.VMEM((4, TOK, w), BF16) for w in widths]
    for _ in range(3):
        scratch += [pltpu.VMEM((4, 4, ROWS, w), BF16) for w in widths]
    scratch += [pltpu.VMEM((4, TOK, w), BF16) for w in widths]
    scratch += [
        dma((6,)), dma((3,)), dma((3,)), dma, dma, dma((10,)), dma((10,)),
        dma((3, 4)), dma((3, 4)), dma((3, 4)), dma((3, 4)), dma((3, 4, 4)), dma((3, 4, 4)),
        dma((3, 4, 4)), dma((3, 4, 4)), dma((3, 4)), dma((3, 4)), dma((3, 4)), dma((3, 4)),
        pltpu.SemaphoreType.REGULAR((3, 4)),
    ]
    return pl.pallas_call(
        expert_kernel,
        out_shape=(
            jax.ShapeDtypeStruct((TOK, HQ * HD), BF16),
            jax.ShapeDtypeStruct((TOK, D), BF16),
        ),
        in_specs=[vmem, vmem, vmem, vmem, vmem, smem] + [hbm] * 6,
        out_specs=(vmem, vmem),
        scratch_shapes=scratch,
        compiler_params=pltpu.CompilerParams(
            collective_id=1, has_side_effects=True, vmem_limit_bytes=62 << 20
        ),
        name="experts_and_attention",
    )(hidden, again, egain, routes, rweight, lengths, queries, kproj, vproj, gate, up, down)


def layer_norm(values, gain):
    mean_value = jnp.mean(values, axis=-1, keepdims=True)
    centered = values - mean_value
    variance = jnp.mean(centered * centered, axis=-1, keepdims=True)
    return centered * lax.rsqrt(variance + EPSILON) * gain


def local(
    patches,
    vision_gain,
    vision_up,
    vision_down,
    merger,
    visual_spots,
    text_embed,
    queries,
    attention_gain,
    key_proj,
    value_proj,
    prompt_lengths,
    expert_gain,
    routes,
    route_weight,
    gate_weight,
    up_weight,
    down_weight,
):
    wide_count = lax.axis_size("wide")
    narrow_count = lax.axis_size("narrow")
    narrow_index = lax.axis_index("narrow")
    patch_rows = patches.astype(jnp.float32)
    normed = layer_norm(patch_rows, vision_gain).astype(jnp.bfloat16)
    inner_act = jax.nn.gelu(
        jnp.dot(normed, vision_up, preferred_element_type=jnp.float32), approximate=True
    ).astype(jnp.bfloat16)
    partial_out = jnp.dot(inner_act, vision_down, preferred_element_type=jnp.float32)
    summed = lax.psum(partial_out, "narrow")
    vision_out = (patch_rows + summed).astype(jnp.bfloat16)
    visual_dev = vision_out.shape[0] // MERGE
    merged = vision_out.reshape(visual_dev, MERGE * vision_out.shape[1])
    visual = jnp.dot(merged, merger, preferred_element_type=jnp.float32).astype(jnp.bfloat16)
    device_total = wide_count * narrow_count
    per_dest = visual_dev // device_total
    half_width = visual.shape[1]
    outgoing = visual.reshape(device_total, per_dest, half_width)
    spot_out = visual_spots.reshape(device_total, per_dest, 1)
    arrived, spot_in = (
        lax.all_to_all(outgoing, ("wide", "narrow"), split_axis=0, concat_axis=2, tiled=True),
        lax.all_to_all(spot_out, ("wide", "narrow"), split_axis=0, concat_axis=2, tiled=True),
    )
    arrived = arrived.reshape(per_dest * wide_count, narrow_count * half_width)
    spot_list = spot_in.reshape(per_dest, wide_count, narrow_count)[:, :, 0].reshape(-1)
    tok_dev = text_embed.shape[0]
    visual_flag = jnp.zeros((tok_dev,), jnp.float32).at[spot_list].set(1.0)
    placed = jnp.zeros_like(text_embed).at[spot_list].set(arrived)
    hidden = jnp.where(visual_flag[:, None] > 0.5, placed, text_embed)
    return experts_and_attention(
        hidden, attention_gain.reshape(1, -1), expert_gain.reshape(1, -1), routes.T, route_weight.T,
        prompt_lengths, queries, key_proj, value_proj, gate_weight, up_weight, down_weight,
    )


def solution(mesh):
    return jax.shard_map(
        local,
        mesh=mesh,
        in_specs=(
            P("wide", None),
            P(),
            P(None, "narrow"),
            P("narrow", None),
            P(None, "narrow"),
            P("wide"),
            P(("wide", "narrow"), None),
            P(("wide", "narrow"), None),
            P(),
            P(),
            P(),
            P("wide"),
            P(),
            P(("wide", "narrow"), None),
            P(("wide", "narrow"), None),
            P("wide", None, "narrow"),
            P("wide", None, "narrow"),
            P("wide", "narrow", None),
        ),
        out_specs=(P(("wide", "narrow"), None), P(("wide", "narrow"), None)),
        check_vma=False,
    )
```

```python
import functools

import jax
import jax.numpy as jnp
from jax import lax
from jax.experimental import pallas as pl
from jax.experimental.pallas import tpu as pltpu
from jax.sharding import PartitionSpec as P

MERGE = 4
HQ = 32
KVH = 2
HD = 128
D = 2048
FE = 768
HALF = FE // 2
CAP = 24
TOK = 128
LINE = 4
ROWS = LINE * CAP
EPSILON = 1e-06
MESH = pl.DeviceIdType.MESH
BF16 = jnp.bfloat16
F32 = jnp.float32

SLICES = ((0, 640), (640, 640), (1280, 768))
ORDERS = ((0, 1, 2), (1, 2, 0), (2, 0, 1))
FAR_FIRST = (2, 1, 3)


def wide_of(place):
    return place[0] * 16 + place[1] * 4 + place[2]


def shifted(place, axis, step):
    moved = list(place)
    moved[axis] = lax.rem(place[axis] + step + 4, 4)
    return tuple(moved)


def source_index(order, ka, kb, kc):
    offset = [0, 0, 0]
    offset[order[0]], offset[order[1]], offset[order[2]] = ka, kb, kc
    return offset[0] * 16 + offset[1] * 4 + offset[2]


def lane_iota(shape, dim):
    return lax.broadcasted_iota(jnp.int32, shape, dim)


def expert_kernel(
    hidden_ref, again_ref, egain_ref, routes_ref, rweight_ref, length_ref,
    queries_hbm, kproj_hbm, vproj_hbm, gate_hbm, up_hbm, down_hbm,
    attended_ref, mix_ref,
    gu, dn, acc, part, queries, kproj, vproj, kv, tables,
    g0, g1, g2, tx0, tx1, tx2, mid0, mid1, mid2, rx0, rx1, rx2, fin0, fin1, fin2,
    local_sem, wsend, wrecv, kvsend, kvrecv, tsend, trecv,
    s1send, s1recv, s2send, s2recv, s3send, s3recv,
    r1send, r1recv, r2send, r2recv, r3send, r3recv, free_sem,
):
    gs, txs, mids, rxs, fins = (
        (g0, g1, g2), (tx0, tx1, tx2), (mid0, mid1, mid2), (rx0, rx1, rx2), (fin0, fin1, fin2)
    )
    wide = lax.axis_index("wide")
    narrow = lax.axis_index("narrow")
    place = (wide // 16, lax.rem(wide // 4, 4), lax.rem(wide, 4))

    def peer(axis, step):
        return (wide_of(shifted(place, axis, step)), narrow)

    partner = (wide, 1 - narrow)
    barrier = pltpu.get_barrier_semaphore()
    for axis in range(3):
        for step in (1, 2, 3):
            pl.semaphore_signal(barrier, inc=1, device_id=peer(axis, step), device_id_type=MESH)
    pl.semaphore_signal(barrier, inc=1, device_id=partner, device_id_type=MESH)

    def remote(src, dst, send, recv, device):
        return pltpu.make_async_remote_copy(
            src_ref=src, dst_ref=dst, send_sem=send, recv_sem=recv, device_id=device,
            device_id_type=MESH,
        )

    loads = [
        pltpu.make_async_copy(kproj_hbm, kproj, local_sem.at[0]),
        pltpu.make_async_copy(vproj_hbm, vproj, local_sem.at[1]),
        pltpu.make_async_copy(queries_hbm, queries, local_sem.at[2]),
        pltpu.make_async_copy(gate_hbm.at[0], gu.at[:, 0:HALF], local_sem.at[3]),
        pltpu.make_async_copy(up_hbm.at[0], gu.at[:, FE:FE + HALF], local_sem.at[4]),
        pltpu.make_async_copy(down_hbm.at[0], dn.at[0:HALF, :], local_sem.at[5]),
    ]
    for load in loads:
        load.start()

    expert_iota = lane_iota((64, TOK), 0)
    member = jnp.zeros((64, TOK), F32)
    weight = jnp.zeros((64, TOK), F32)
    for k in range(8):
        hit = routes_ref[k:k + 1, :] == expert_iota
        member = member + jnp.where(hit, 1.0, 0.0)
        weight = weight + jnp.where(hit, rweight_ref[k:k + 1, :], 0.0)
    before = (lane_iota((TOK, TOK), 0) < lane_iota((TOK, TOK), 1)).astype(F32).astype(BF16)
    rank = jnp.dot(member.astype(BF16), before, preferred_element_type=F32)
    tables[0, 0] = jnp.where(member > 0.5, rank, -1.0)
    tables[0, 1] = weight

    hidden = hidden_ref[...].astype(F32)
    scale = lax.rsqrt(jnp.mean(hidden * hidden, axis=-1, keepdims=True) + EPSILON)
    scaled = hidden * scale
    moe_in = (scaled * egain_ref[...]).astype(BF16)
    attn_in = (scaled * again_ref[...]).astype(BF16)
    for s, (start, width) in enumerate(SLICES):
        gs[s][0] = moe_in[:, start:start + width]

    pl.semaphore_wait(barrier, 10)

    table_copies = []
    hop1 = {}
    for axis in range(3):
        for step in (1, 2, 3):
            slot = 1 + axis * 3 + step - 1
            copy = remote(
                tables.at[0], tables.at[slot], tsend.at[slot], trecv.at[slot], peer(axis, step)
            )
            copy.start()
            table_copies.append(copy)
    for s in range(3):
        for k in FAR_FIRST:
            copy = remote(
                gs[s].at[0], gs[s].at[k], s1send.at[s, k], s1recv.at[s, k], peer(ORDERS[s][0], k)
            )
            copy.start()
            hop1[s, k] = copy

    loads[0].wait()
    loads[1].wait()
    own_keys = jnp.dot(attn_in, kproj[...], preferred_element_type=F32).astype(BF16)
    own_values = jnp.dot(attn_in, vproj[...], preferred_element_type=F32).astype(BF16)
    kv[narrow, :, 0:KVH * HD] = own_keys
    kv[narrow, :, KVH * HD:] = own_values
    kv_copy = remote(kv.at[narrow], kv.at[narrow], kvsend, kvrecv, partner)
    kv_copy.start()
    weight_copies = [
        remote(gate_hbm.at[0], gu.at[:, HALF:FE], wsend.at[0], wrecv.at[0], partner),
        remote(up_hbm.at[0], gu.at[:, FE + HALF:], wsend.at[1], wrecv.at[1], partner),
        remote(down_hbm.at[0], dn.at[HALF:, :], wsend.at[2], wrecv.at[2], partner),
    ]
    for copy in weight_copies:
        copy.start()

    slot_iota = lane_iota((ROWS, LINE * TOK), 0).astype(F32)

    def slot_blocks(s, kb, weighted):
        axis_a, axis_b, axis_c = ORDERS[s]
        blocks = []
        for kc in range(4):
            expert = wide_of(shifted(shifted(place, axis_b, kb), axis_c, kc))
            rows = []
            weights = []
            for ka in range(4):
                slot = 0 if ka == 0 else 1 + axis_a * 3 + ka - 1
                row = tables[slot, 0, pl.ds(expert, 1), :]
                rows.append(jnp.where(row >= 0.0, row + float(CAP * ka), -1.0))
                if weighted:
                    weights.append(tables[slot, 1, pl.ds(expert, 1), :])
            hit = slot_iota == jnp.concatenate(rows, axis=1)
            if weighted:
                value = jnp.where(hit, jnp.concatenate(weights, axis=1), 0.0)
            else:
                value = jnp.where(hit, 1.0, 0.0)
            blocks.append(value.astype(BF16))
        return jnp.concatenate(blocks, axis=0)

    for copy in table_copies:
        copy.wait_recv()

    hop2 = {}
    for s, (start, width) in enumerate(SLICES):
        for k in (1, 2, 3):
            hop1[s, k].wait_recv()
    for kb in (2, 1, 3, 0):
        for s, (start, width) in enumerate(SLICES):
            tokens = gs[s][...].reshape(LINE * TOK, width)
            rows = jnp.dot(slot_blocks(s, kb, False), tokens, preferred_element_type=F32)
            rows = rows.astype(BF16).reshape(4, ROWS, width)
            if kb == 0:
                mids[s][0] = rows
            else:
                txs[s][kb] = rows
                copy = remote(
                    txs[s].at[kb], mids[s].at[kb], s2send.at[s, kb], s2recv.at[s, kb],
                    peer(ORDERS[s][1], kb),
                )
                copy.start()
                hop2[s, kb] = copy

    hop3 = {}

    def forward(kb):
        for s in range(3):
            if kb:
                hop2[s, kb].wait_recv()
            for kc in FAR_FIRST:
                copy = remote(
                    mids[s].at[kb, kc], rxs[s].at[kc, kb], s3send.at[s, kc, kb],
                    s3recv.at[s, kc, kb], peer(ORDERS[s][2], kc),
                )
                copy.start()
                hop3[s, kc, kb] = copy

    forward(0)

    kv_copy.wait_recv()
    loads[2].wait()
    row_pos = lane_iota((TOK, 2 * TOK), 0) + narrow * TOK
    key_pos = lane_iota((TOK, 2 * TOK), 1)
    limit = jnp.minimum(row_pos, length_ref[0] - 1)
    allowed = key_pos <= limit

    def attend(head, group):
        columns = pl.ds(pl.multiple_of(head * HD, HD), HD)
        keys = kv[:, :, group * HD:(group + 1) * HD].reshape(2 * TOK, HD)
        values = kv[:, :, (KVH + group) * HD:(KVH + group + 1) * HD].reshape(2 * TOK, HD)
        scores = lax.dot_general(
            queries[:, columns], keys, (((1,), (1,)), ((), ())), preferred_element_type=F32
        ) * HD ** (-0.5)
        scores = jnp.where(allowed, scores, -1e30)
        row_max = jnp.max(scores, axis=-1, keepdims=True)
        weights = jnp.exp(scores - row_max)
        total = jnp.sum(weights, axis=-1, keepdims=True)
        mixed = jnp.dot(weights.astype(BF16), values, preferred_element_type=F32)
        attended_ref[:, columns] = (mixed / total).astype(BF16)

    group_size = HQ // KVH

    def attend_heads(first, count, group):
        def body(i, carry):
            for j in range(4):
                attend(first + i * 4 + j, group)
            return carry
        lax.fori_loop(0, count // 4, body, 0)

    attend_heads(0, 16, 0)
    forward(1)
    forward(3)
    attend_heads(16, 16, 1)
    for copy in hop2.values():
        copy.wait_send()
    forward(2)

    for load in loads[3:]:
        load.wait()
    for copy in weight_copies:
        copy.wait_recv()

    written = set()

    def project(s, kc):
        start, width = SLICES[s]
        if kc:
            for kb in range(4):
                hop3[s, kc, kb].wait_recv()
            rows = rxs[s][kc].reshape(4 * ROWS, width)
        else:
            rows = mids[s][:, 0].reshape(4 * ROWS, width)
        for n in range(2):
            out = jnp.dot(
                rows, gu[start:start + width, n * FE:(n + 1) * FE], preferred_element_type=F32
            ).reshape(4, 4, CAP, FE)
            for kb in range(4):
                for ka in range(4):
                    index = source_index(ORDERS[s], ka, kb, kc)
                    if (n, index) in written:
                        acc[index, :, n * FE:(n + 1) * FE] += out[kb, ka]
                    else:
                        written.add((n, index))
                        acc[index, :, n * FE:(n + 1) * FE] = out[kb, ka]

    for kc in (0, 1, 3, 2):
        for s in range(3):
            project(s, kc)

    def activate(i, carry):
        gate = acc[i, :, 0:FE]
        up = acc[i, :, FE:]
        acc[i, :, 0:FE] = gate * (1.0 / (1.0 + jnp.exp(-gate))) * up
        return carry

    lax.fori_loop(0, 64, activate, 0)

    for copy in hop3.values():
        copy.wait_send()
    for s in range(3):
        for kb in (1, 2, 3):
            pl.semaphore_signal(
                free_sem.at[s, kb], inc=1, device_id=peer(ORDERS[s][1], kb), device_id_type=MESH
            )

    back1 = {}
    for kc in (2, 1, 3, 0):
        for s, (start, width) in enumerate(SLICES):
            pieces = [
                acc[source_index(ORDERS[s], ka, kb, kc), :, 0:FE]
                for kb in range(4) for ka in range(4)
            ]
            active = jnp.concatenate(pieces, axis=0).astype(BF16)
            out = jnp.dot(active, dn[:, start:start + width], preferred_element_type=F32)
            out = out.astype(BF16).reshape(4, ROWS, width)
            if kc == 0:
                txs[s][:, 0] = out
            else:
                rxs[s][kc] = out
                for kb in (2, 1, 3, 0):
                    copy = remote(
                        rxs[s].at[kc, kb], txs[s].at[kb, kc], r1send.at[s, kc, kb],
                        r1recv.at[s, kc, kb], peer(ORDERS[s][2], -kc),
                    )
                    copy.start()
                    back1[s, kc, kb] = copy

    back2 = {}
    for kb in (2, 1, 3, 0):
        for s in range(3):
            for kc in (2, 1, 3):
                back1[s, kc, kb].wait_recv()
            if kb:
                pl.semaphore_wait(free_sem.at[s, kb], 1)
                copy = remote(
                    txs[s].at[kb], mids[s].at[kb], r2send.at[s, kb], r2recv.at[s, kb],
                    peer(ORDERS[s][1], -kb),
                )
                copy.start()
                back2[s, kb] = copy

    for kb in (0, 1, 3, 2):
        for s, (start, width) in enumerate(SLICES):
            if kb:
                back2[s, kb].wait_recv()
                rows = mids[s][kb].reshape(4 * ROWS, width)
            else:
                rows = txs[s][0].reshape(4 * ROWS, width)
            total = lax.dot_general(
                slot_blocks(s, kb, True), rows, (((0,), (0,)), ((), ())),
                preferred_element_type=F32,
            )
            if kb:
                part[:, start:start + width] += total
            else:
                part[:, start:start + width] = total

    back3 = {}
    for s, (start, width) in enumerate(SLICES):
        for k in FAR_FIRST:
            gs[s][k] = part[k * TOK:(k + 1) * TOK, start:start + width].astype(BF16)
            copy = remote(
                gs[s].at[k], fins[s].at[k], r3send.at[s, k], r3recv.at[s, k],
                peer(ORDERS[s][0], -k),
            )
            copy.start()
            back3[s, k] = copy
    for s, (start, width) in enumerate(SLICES):
        total = part[0:TOK, start:start + width]
        for k in (1, 3, 2):
            back3[s, k].wait_recv()
            total = total + fins[s][k].astype(F32)
        mix_ref[:, start:start + width] = total.astype(BF16)

    kv_copy.wait_send()
    for copies in (table_copies, weight_copies, hop1.values(), back1.values(), back2.values(),
                   back3.values()):
        for copy in copies:
            copy.wait_send()


def experts_and_attention(
    hidden, again, egain, routes, rweight, lengths, queries, kproj, vproj, gate, up, down
):
    vmem = pl.BlockSpec(memory_space=pltpu.VMEM)
    smem = pl.BlockSpec(memory_space=pltpu.SMEM)
    hbm = pl.BlockSpec(memory_space=pl.ANY)
    dma = pltpu.SemaphoreType.DMA
    widths = [width for _, width in SLICES]
    scratch = [
        pltpu.VMEM((D, 2 * FE), BF16),
        pltpu.VMEM((FE, D), BF16),
        pltpu.VMEM((64, CAP, 2 * FE), F32),
        pltpu.VMEM((LINE * TOK, D), F32),
        pltpu.VMEM((TOK, HQ * HD), BF16),
        pltpu.VMEM((D, KVH * HD), BF16),
        pltpu.VMEM((D, KVH * HD), BF16),
        pltpu.VMEM((2, TOK, 2 * KVH * HD), BF16),
        pltpu.VMEM((10, 2, 64, TOK), F32),
    ]
    scratch += [pltpu.VMEM((4, TOK, w), BF16) for w in widths]
    for _ in range(3):
        scratch += [pltpu.VMEM((4, 4, ROWS, w), BF16) for w in widths]
    scratch += [pltpu.VMEM((4, TOK, w), BF16) for w in widths]
    scratch += [
        dma((6,)), dma((3,)), dma((3,)), dma, dma, dma((10,)), dma((10,)),
        dma((3, 4)), dma((3, 4)), dma((3, 4)), dma((3, 4)), dma((3, 4, 4)), dma((3, 4, 4)),
        dma((3, 4, 4)), dma((3, 4, 4)), dma((3, 4)), dma((3, 4)), dma((3, 4)), dma((3, 4)),
        pltpu.SemaphoreType.REGULAR((3, 4)),
    ]
    return pl.pallas_call(
        expert_kernel,
        out_shape=(
            jax.ShapeDtypeStruct((TOK, HQ * HD), BF16),
            jax.ShapeDtypeStruct((TOK, D), BF16),
        ),
        in_specs=[vmem, vmem, vmem, vmem, vmem, smem] + [hbm] * 6,
        out_specs=(vmem, vmem),
        scratch_shapes=scratch,
        compiler_params=pltpu.CompilerParams(
            collective_id=1, has_side_effects=True, vmem_limit_bytes=62 << 20
        ),
        name="experts_and_attention",
    )(hidden, again, egain, routes, rweight, lengths, queries, kproj, vproj, gate, up, down)


DV = 1152
FH = 1152
N_WIDE = 64


def vision_kernel(
    patches_ref, gain_ref, spots_ref, text_ref, up_hbm, down_hbm, merger_hbm,
    hidden_ref,
    up, down, merger, ordered, own, psend, precv, half_send, half_recv, rows_f, rows, arrived,
    arrived_f, spots,
    local_sem, psend_sem, precv_sem, hsend_sem, hrecv_sem, ssend, srecv, rsend, rrecv,
):
    wide = lax.axis_index("wide")
    narrow = lax.axis_index("narrow")
    place = (wide // 16, lax.rem(wide // 4, 4), lax.rem(wide, 4))
    partner = (wide, 1 - narrow)

    def peer(axis, step):
        return (wide_of(shifted(place, axis, step)), narrow)

    def offset_wide(k):
        return wide_of(
            shifted(shifted(shifted(place, 0, k // 16), 1, lax.rem(k // 4, 4)), 2, lax.rem(k, 4))
        )

    def remote(src, dst, send, recv, device):
        return pltpu.make_async_remote_copy(
            src_ref=src, dst_ref=dst, send_sem=send, recv_sem=recv, device_id=device,
            device_id_type=MESH,
        )

    loads = [
        pltpu.make_async_copy(up_hbm, up, local_sem.at[0]),
        pltpu.make_async_copy(down_hbm, down, local_sem.at[1]),
        pltpu.make_async_copy(merger_hbm, merger, local_sem.at[2]),
    ]
    for load in loads:
        load.start()
    barrier = pltpu.get_barrier_semaphore()
    pl.semaphore_signal(barrier, inc=1, device_id=partner, device_id_type=MESH)

    def greet(k, carry):
        pl.semaphore_signal(
            barrier, inc=1, device_id=(offset_wide(k), narrow), device_id_type=MESH
        )
        return carry

    lax.fori_loop(1, N_WIDE, greet, 0)

    row = lane_iota((4 * TOK, 4 * TOK), 0)
    order = (lane_iota((4 * TOK, 4 * TOK), 1) == 4 * lax.rem(row, TOK) + row // TOK)
    order = jnp.where(order, 1.0, 0.0).astype(BF16)
    ordered[...] = jnp.dot(order, patches_ref[...], preferred_element_type=F32)
    spots[0, 0, 0] = jnp.broadcast_to(spots_ref[...], (8, TOK)).astype(F32)

    def spot_hop(axis):
        copies = []
        for k in (2, 1, 3):
            if axis == 0:
                src, dst = spots.at[0, 0, 0], spots.at[k, 0, 0]
            elif axis == 1:
                src, dst = spots.at[:, 0, 0], spots.at[:, k, 0]
            else:
                src, dst = spots.at[:, :, 0], spots.at[:, :, k]
            copy = remote(src, dst, ssend.at[axis, k], srecv.at[axis, k], peer(axis, k))
            copy.start()
            copies.append(copy)
        return copies

    halves = []
    spot_copies = []
    for m in range(MERGE):
        patch = ordered[m * TOK:(m + 1) * TOK]
        mean = jnp.mean(patch, axis=-1, keepdims=True)
        centered = patch - mean
        variance = jnp.mean(centered * centered, axis=-1, keepdims=True)
        normed = (centered * lax.rsqrt(variance + EPSILON) * gain_ref[...]).astype(BF16)
        if m == 0:
            loads[0].wait()
        inner = jnp.dot(normed, up[...], preferred_element_type=F32)
        inner = jax.nn.gelu(inner, approximate=True).astype(BF16)
        if m == 0:
            loads[1].wait()
        partial = jnp.dot(inner, down[...], preferred_element_type=F32)
        own[m] = patch + partial
        psend[m] = partial.astype(BF16)
        if m == 0:
            pl.semaphore_wait(barrier, N_WIDE)
        copy = remote(psend.at[m], precv.at[m], psend_sem.at[m], precv_sem.at[m], partner)
        copy.start()
        halves.append(copy)
        if m < 3:
            for copy in spot_copies[3 * (m - 1):]:
                copy.wait_recv()
            spot_copies += spot_hop(m)

    loads[2].wait()
    visual = jnp.zeros((TOK, D // 2), F32)
    for m in range(MERGE):
        halves[m].wait_recv()
        merged = (own[m] + precv[m].astype(F32)).astype(BF16)
        visual = visual + jnp.dot(
            merged, merger[m * DV:(m + 1) * DV], preferred_element_type=F32
        )
    visual = visual.astype(BF16)

    row = lane_iota((TOK, TOK), 0)
    wanted = 2 * lax.rem(row, N_WIDE) + jnp.where(row < N_WIDE, narrow, 1 - narrow)
    choose = jnp.where(lane_iota((TOK, TOK), 1) == wanted, 1.0, 0.0).astype(BF16)
    sorted_rows = jnp.dot(choose, visual, preferred_element_type=F32)
    half_send[...] = sorted_rows[N_WIDE:].astype(BF16)
    half_copy = remote(half_send, half_recv, hsend_sem, hrecv_sem, partner)
    half_copy.start()
    for j in range(8):
        rows_f[:, narrow, j, :] = sorted_rows[:N_WIDE, j * TOK:(j + 1) * TOK]
    half_copy.wait_recv()
    other = half_recv[...].astype(F32)
    for j in range(8):
        rows_f[:, 1 - narrow, j, :] = other[:, j * TOK:(j + 1) * TOK]
    rows[...] = rows_f[...].reshape(N_WIDE, 16, TOK).astype(BF16)

    def row_copy(k):
        target = offset_wide(k)
        return remote(rows.at[target], arrived.at[k], rsend.at[k], rrecv.at[k], (target, narrow))

    def start_row(k, carry):
        row_copy(k).start()
        return carry

    def wait_row(k, carry):
        row_copy(k).wait()
        return carry

    lax.fori_loop(1, N_WIDE, start_row, 0, unroll=7)
    arrived[0] = rows[wide]
    for copy in spot_copies[6:]:
        copy.wait_recv()
    spot_rows = spots[...].reshape(N_WIDE, 8, TOK)[:, 0, :]
    lane = lane_iota((N_WIDE, TOK), 1)
    spot = jnp.sum(jnp.where(lane == 2 * wide + narrow, spot_rows, 0.0), axis=1, keepdims=True)
    put = jnp.where(lane.astype(F32) == spot, 1.0, 0.0).astype(BF16)
    flag = lax.dot_general(
        put, jnp.ones((N_WIDE, TOK), BF16), (((0,), (0,)), ((), ())), preferred_element_type=F32
    )[:, 0:1]
    lax.fori_loop(1, N_WIDE, wait_row, 0, unroll=7)
    arrived_f[...] = arrived[...].astype(F32)
    columns = jnp.concatenate([arrived_f[:, j, :] for j in range(16)], axis=1).astype(BF16)
    placed = lax.dot_general(put, columns, (((0,), (0,)), ((), ())), preferred_element_type=F32)
    hidden_ref[...] = jnp.where(flag > 0.5, placed, text_ref[...].astype(F32)).astype(BF16)

    half_copy.wait_send()
    for copies in (halves, spot_copies):
        for copy in copies:
            copy.wait_send()


def vision_and_placement(patches, gain, spots, text, up, down, merger):
    vmem = pl.BlockSpec(memory_space=pltpu.VMEM)
    hbm = pl.BlockSpec(memory_space=pl.ANY)
    dma = pltpu.SemaphoreType.DMA
    return pl.pallas_call(
        vision_kernel,
        out_shape=jax.ShapeDtypeStruct((TOK, D), BF16),
        in_specs=[vmem] * 4 + [hbm] * 3,
        out_specs=vmem,
        scratch_shapes=[
            pltpu.VMEM((DV, FH), BF16),
            pltpu.VMEM((FH, DV), BF16),
            pltpu.VMEM((MERGE * DV, D // 2), BF16),
            pltpu.VMEM((MERGE * TOK, DV), F32),
            pltpu.VMEM((MERGE, TOK, DV), F32),
            pltpu.VMEM((MERGE, TOK, DV), BF16),
            pltpu.VMEM((MERGE, TOK, DV), BF16),
            pltpu.VMEM((N_WIDE, D // 2), BF16),
            pltpu.VMEM((N_WIDE, D // 2), BF16),
            pltpu.VMEM((N_WIDE, 2, 8, TOK), F32),
            pltpu.VMEM((N_WIDE, 16, TOK), BF16),
            pltpu.VMEM((N_WIDE, 16, TOK), BF16),
            pltpu.VMEM((N_WIDE, 16, TOK), F32),
            pltpu.VMEM((4, 4, 4, 8, TOK), F32),
            dma((3,)), dma((4,)), dma((4,)), dma, dma, dma((3, 4)), dma((3, 4)),
            dma((N_WIDE,)), dma((N_WIDE,)),
        ],
        compiler_params=pltpu.CompilerParams(
            collective_id=0, has_side_effects=True, vmem_limit_bytes=56 << 20
        ),
        name="vision_and_placement",
    )(patches, gain, spots, text, up, down, merger)


def local(
    patches,
    vision_gain,
    vision_up,
    vision_down,
    merger,
    visual_spots,
    text_embed,
    queries,
    attention_gain,
    key_proj,
    value_proj,
    prompt_lengths,
    expert_gain,
    routes,
    route_weight,
    gate_weight,
    up_weight,
    down_weight,
):
    hidden = vision_and_placement(
        patches, vision_gain.reshape(1, -1), visual_spots.reshape(1, -1), text_embed, vision_up,
        vision_down, merger,
    )
    return experts_and_attention(
        hidden, attention_gain.reshape(1, -1), expert_gain.reshape(1, -1), routes.T, route_weight.T,
        prompt_lengths, queries, key_proj, value_proj, gate_weight, up_weight, down_weight,
    )


def solution(mesh):
    return jax.shard_map(
        local,
        mesh=mesh,
        in_specs=(
            P("wide", None),
            P(),
            P(None, "narrow"),
            P("narrow", None),
            P(None, "narrow"),
            P("wide"),
            P(("wide", "narrow"), None),
            P(("wide", "narrow"), None),
            P(),
            P(),
            P(),
            P("wide"),
            P(),
            P(("wide", "narrow"), None),
            P(("wide", "narrow"), None),
            P("wide", None, "narrow"),
            P("wide", None, "narrow"),
            P("wide", "narrow", None),
        ),
        out_specs=(P(("wide", "narrow"), None), P(("wide", "narrow"), None)),
        check_vma=False,
    )
```

```python
import functools

import jax
import jax.numpy as jnp
from jax import lax
from jax.experimental import pallas as pl
from jax.experimental.pallas import tpu as pltpu
from jax.sharding import PartitionSpec as P

MERGE = 4
HQ = 32
KVH = 2
HD = 128
D = 2048
FE = 768
HALF = FE // 2
CAP = 24
TOK = 128
LINE = 4
PARTS = ((0, 16), (16, 8))
EPSILON = 1e-06
MESH = pl.DeviceIdType.MESH
BF16 = jnp.bfloat16
F32 = jnp.float32

SLICES = ((0, 640), (640, 640), (1280, 768))
ORDERS = ((0, 1, 2), (1, 2, 0), (2, 0, 1))
NEAR_FIRST = (1, 3, 2)


def wide_of(place):
    return place[0] * 16 + place[1] * 4 + place[2]


def shifted(place, axis, step):
    moved = list(place)
    moved[axis] = lax.rem(place[axis] + step + 4, 4)
    return tuple(moved)


def source_index(order, ka, kb, kc):
    offset = [0, 0, 0]
    offset[order[0]], offset[order[1]], offset[order[2]] = ka, kb, kc
    return offset[0] * 16 + offset[1] * 4 + offset[2]


def lane_iota(shape, dim):
    return lax.broadcasted_iota(jnp.int32, shape, dim)


def expert_kernel(
    hidden_ref, again_ref, egain_ref, routes_ref, rweight_ref, length_ref,
    queries_hbm, kproj_hbm, vproj_hbm, gate_hbm, up_hbm, down_hbm,
    attended_ref, mix_ref,
    gu, dn, acc0, acc1, part, queries, kproj, vproj, kv, tables,
    g0, g1, g2, fin0, fin1, fin2,
    tx00, tx01, tx02, tx10, tx11, tx12, mid00, mid01, mid02, mid10, mid11, mid12,
    rx00, rx01, rx02, rx10, rx11, rx12,
    local_sem, wsend, wrecv, kvsend, kvrecv, tsend, trecv,
    s1send, s1recv, s2send, s2recv, s3send, s3recv,
    r1send, r1recv, r2send, r2recv, r3send, r3recv, free_sem,
):
    gs, fins, accs = (g0, g1, g2), (fin0, fin1, fin2), (acc0, acc1)
    txs = ((tx00, tx01, tx02), (tx10, tx11, tx12))
    mids = ((mid00, mid01, mid02), (mid10, mid11, mid12))
    rxs = ((rx00, rx01, rx02), (rx10, rx11, rx12))
    wide = lax.axis_index("wide")
    narrow = lax.axis_index("narrow")
    place = (wide // 16, lax.rem(wide // 4, 4), lax.rem(wide, 4))

    def peer(axis, step):
        return (wide_of(shifted(place, axis, step)), narrow)

    partner = (wide, 1 - narrow)
    barrier = pltpu.get_barrier_semaphore()
    for axis in range(3):
        for step in (1, 2, 3):
            pl.semaphore_signal(barrier, inc=1, device_id=peer(axis, step), device_id_type=MESH)
    pl.semaphore_signal(barrier, inc=1, device_id=partner, device_id_type=MESH)

    def remote(src, dst, send, recv, device):
        return pltpu.make_async_remote_copy(
            src_ref=src, dst_ref=dst, send_sem=send, recv_sem=recv, device_id=device,
            device_id_type=MESH,
        )

    loads = [
        pltpu.make_async_copy(kproj_hbm, kproj, local_sem.at[0]),
        pltpu.make_async_copy(vproj_hbm, vproj, local_sem.at[1]),
        pltpu.make_async_copy(queries_hbm, queries, local_sem.at[2]),
        pltpu.make_async_copy(gate_hbm.at[0], gu.at[:, 0:HALF], local_sem.at[3]),
        pltpu.make_async_copy(up_hbm.at[0], gu.at[:, FE:FE + HALF], local_sem.at[4]),
        pltpu.make_async_copy(down_hbm.at[0], dn.at[0:HALF, :], local_sem.at[5]),
    ]
    for load in loads:
        load.start()

    expert_iota = lane_iota((64, TOK), 0)
    member = jnp.zeros((64, TOK), F32)
    weight = jnp.zeros((64, TOK), F32)
    for k in range(8):
        hit = routes_ref[k:k + 1, :] == expert_iota
        member = member + jnp.where(hit, 1.0, 0.0)
        weight = weight + jnp.where(hit, rweight_ref[k:k + 1, :], 0.0)
    before = (lane_iota((TOK, TOK), 0) < lane_iota((TOK, TOK), 1)).astype(F32).astype(BF16)
    rank = jnp.dot(member.astype(BF16), before, preferred_element_type=F32)
    tables[0, 0] = jnp.where(member > 0.5, rank, -1.0)
    tables[0, 1] = weight

    hidden = hidden_ref[...].astype(F32)
    scale = lax.rsqrt(jnp.mean(hidden * hidden, axis=-1, keepdims=True) + EPSILON)
    scaled = hidden * scale
    moe_in = (scaled * egain_ref[...]).astype(BF16)
    attn_in = (scaled * again_ref[...]).astype(BF16)
    for s, (start, width) in enumerate(SLICES):
        gs[s][0] = moe_in[:, start:start + width]

    pl.semaphore_wait(barrier, 10)

    table_copies = []
    hop1 = {}
    for axis in range(3):
        for step in (1, 2, 3):
            slot = 1 + axis * 3 + step - 1
            copy = remote(
                tables.at[0], tables.at[slot], tsend.at[slot], trecv.at[slot], peer(axis, step)
            )
            copy.start()
            table_copies.append(copy)
    for s in range(3):
        for k in NEAR_FIRST:
            copy = remote(
                gs[s].at[0], gs[s].at[k], s1send.at[s, k], s1recv.at[s, k], peer(ORDERS[s][0], k)
            )
            copy.start()
            hop1[s, k] = copy

    loads[0].wait()
    loads[1].wait()
    own_keys = jnp.dot(attn_in, kproj[...], preferred_element_type=F32).astype(BF16)
    own_values = jnp.dot(attn_in, vproj[...], preferred_element_type=F32).astype(BF16)
    kv[narrow, :, 0:KVH * HD] = own_keys
    kv[narrow, :, KVH * HD:] = own_values
    kv_copy = remote(kv.at[narrow], kv.at[narrow], kvsend, kvrecv, partner)
    kv_copy.start()
    weight_copies = [
        remote(gate_hbm.at[0], gu.at[:, HALF:FE], wsend.at[0], wrecv.at[0], partner),
        remote(up_hbm.at[0], gu.at[:, FE + HALF:], wsend.at[1], wrecv.at[1], partner),
        remote(down_hbm.at[0], dn.at[HALF:, :], wsend.at[2], wrecv.at[2], partner),
    ]
    for copy in weight_copies:
        copy.start()

    def slot_blocks(p, s, kb, weighted):
        axis_a, axis_b, axis_c = ORDERS[s]
        first, count = PARTS[p]
        slot_iota = lane_iota((LINE * count, LINE * TOK), 0).astype(F32)
        blocks = []
        for kc in range(4):
            expert = wide_of(shifted(shifted(place, axis_b, kb), axis_c, kc))
            rows = []
            weights = []
            for ka in range(4):
                slot = 0 if ka == 0 else 1 + axis_a * 3 + ka - 1
                row = tables[slot, 0, pl.ds(expert, 1), :]
                inside = (row >= float(first)) & (row < float(first + count))
                rows.append(jnp.where(inside, row + float(count * ka - first), -1.0))
                if weighted:
                    weights.append(tables[slot, 1, pl.ds(expert, 1), :])
            hit = slot_iota == jnp.concatenate(rows, axis=1)
            if weighted:
                value = jnp.where(hit, jnp.concatenate(weights, axis=1), 0.0)
            else:
                value = jnp.where(hit, 1.0, 0.0)
            blocks.append(value.astype(BF16))
        return jnp.concatenate(blocks, axis=0)

    for copy in table_copies:
        copy.wait_recv()

    hop2 = {}

    def build(p, kb):
        for s, (start, width) in enumerate(SLICES):
            tokens = gs[s][...].reshape(LINE * TOK, width)
            rows = jnp.dot(slot_blocks(p, s, kb, False), tokens, preferred_element_type=F32)
            rows = rows.astype(BF16).reshape(4, LINE * PARTS[p][1], width)
            if kb == 0:
                mids[p][s][0] = rows
            else:
                txs[p][s][kb] = rows
                copy = remote(
                    txs[p][s].at[kb], mids[p][s].at[kb], s2send.at[p, s, kb],
                    s2recv.at[p, s, kb], peer(ORDERS[s][1], kb),
                )
                copy.start()
                hop2[p, s, kb] = copy

    hop3 = {}

    def forward(p, kb):
        for s in range(3):
            if kb:
                hop2[p, s, kb].wait_recv()
            for kc in NEAR_FIRST:
                copy = remote(
                    mids[p][s].at[kb, kc], rxs[p][s].at[kc, kb], s3send.at[p, s, kc, kb],
                    s3recv.at[p, s, kc, kb], peer(ORDERS[s][2], kc),
                )
                copy.start()
                hop3[p, s, kc, kb] = copy

    def sent(p):
        for (part_of, _, _), copy in hop2.items():
            if part_of == p:
                copy.wait_send()

    def attend(head, group, allowed):
        columns = pl.ds(pl.multiple_of(head * HD, HD), HD)
        keys = kv[:, :, group * HD:(group + 1) * HD].reshape(2 * TOK, HD)
        values = kv[:, :, (KVH + group) * HD:(KVH + group + 1) * HD].reshape(2 * TOK, HD)
        scores = lax.dot_general(
            queries[:, columns], keys, (((1,), (1,)), ((), ())), preferred_element_type=F32
        ) * HD ** (-0.5)
        scores = jnp.where(allowed, scores, -1e30)
        row_max = jnp.max(scores, axis=-1, keepdims=True)
        weights = jnp.exp(scores - row_max)
        total = jnp.sum(weights, axis=-1, keepdims=True)
        mixed = jnp.dot(weights.astype(BF16), values, preferred_element_type=F32)
        attended_ref[:, columns] = (mixed / total).astype(BF16)

    def attend_heads(first, count, group):
        row_pos = lane_iota((TOK, 2 * TOK), 0) + narrow * TOK
        key_pos = lane_iota((TOK, 2 * TOK), 1)
        allowed = key_pos <= jnp.minimum(row_pos, length_ref[0] - 1)

        def body(i, carry):
            for j in range(4):
                attend(first + i * 4 + j, group, allowed)
            return carry
        lax.fori_loop(0, count // 4, body, 0)

    written = set()

    def project(p, kc):
        count = PARTS[p][1]
        for s, (start, width) in enumerate(SLICES):
            if kc:
                for kb in range(4):
                    hop3[p, s, kc, kb].wait_recv()
                rows = rxs[p][s][kc].reshape(16 * count, width)
            else:
                rows = mids[p][s][:, 0].reshape(16 * count, width)
            for n in range(2):
                out = jnp.dot(
                    rows, gu[start:start + width, n * FE:(n + 1) * FE], preferred_element_type=F32
                ).reshape(4, 4, count, FE)
                for kb in range(4):
                    for ka in range(4):
                        index = source_index(ORDERS[s], ka, kb, kc)
                        if (p, n, index) in written:
                            accs[p][index, :, n * FE:(n + 1) * FE] += out[kb, ka]
                        else:
                            written.add((p, n, index))
                            accs[p][index, :, n * FE:(n + 1) * FE] = out[kb, ka]

    def activate(p):
        acc = accs[p]

        def body(i, carry):
            gate = acc[i, :, 0:FE]
            up = acc[i, :, FE:]
            acc[i, :, 0:FE] = gate * (1.0 / (1.0 + jnp.exp(-gate))) * up
            return carry

        lax.fori_loop(0, 64, body, 0)
        for (part_of, _, _, _), copy in hop3.items():
            if part_of == p:
                copy.wait_send()
        for s in range(3):
            for kb in (1, 2, 3):
                pl.semaphore_signal(
                    free_sem.at[p, s, kb], inc=1, device_id=peer(ORDERS[s][1], kb),
                    device_id_type=MESH,
                )

    back1 = {}

    def give_back(p, kc):
        count = PARTS[p][1]
        for s, (start, width) in enumerate(SLICES):
            pieces = [
                accs[p][source_index(ORDERS[s], ka, kb, kc), :, 0:FE]
                for kb in range(4) for ka in range(4)
            ]
            active = jnp.concatenate(pieces, axis=0).astype(BF16)
            out = jnp.dot(active, dn[:, start:start + width], preferred_element_type=F32)
            out = out.astype(BF16).reshape(4, LINE * count, width)
            if kc == 0:
                txs[p][s][:, 0] = out
            else:
                rxs[p][s][kc] = out
                for kb in (1, 3, 2, 0):
                    copy = remote(
                        rxs[p][s].at[kc, kb], txs[p][s].at[kb, kc], r1send.at[p, s, kc, kb],
                        r1recv.at[p, s, kc, kb], peer(ORDERS[s][2], -kc),
                    )
                    copy.start()
                    back1[p, s, kc, kb] = copy

    back2 = {}

    def back(p, kb):
        for s in range(3):
            for kc in NEAR_FIRST:
                back1[p, s, kc, kb].wait_recv()
            if kb:
                pl.semaphore_wait(free_sem.at[p, s, kb], 1)
                copy = remote(
                    txs[p][s].at[kb], mids[p][s].at[kb], r2send.at[p, s, kb],
                    r2recv.at[p, s, kb], peer(ORDERS[s][1], -kb),
                )
                copy.start()
                back2[p, s, kb] = copy

    def combine(p, kb):
        for s, (start, width) in enumerate(SLICES):
            if kb:
                back2[p, s, kb].wait_recv()
                rows = mids[p][s][kb].reshape(16 * PARTS[p][1], width)
            else:
                rows = txs[p][s][0].reshape(16 * PARTS[p][1], width)
            total = lax.dot_general(
                slot_blocks(p, s, kb, True), rows, (((0,), (0,)), ((), ())),
                preferred_element_type=F32,
            )
            if p or kb:
                part[:, start:start + width] += total
            else:
                part[:, start:start + width] = total

    for s in range(3):
        for k in (1, 2, 3):
            hop1[s, k].wait_recv()
    for kb in (1, 3, 2, 0):
        build(0, kb)
    forward(0, 0)
    kv_copy.wait_recv()
    loads[2].wait()
    attend_heads(0, 16, 0)
    forward(0, 1)
    forward(0, 3)
    for kb in (1, 3, 2, 0):
        build(1, kb)
    sent(0)
    forward(0, 2)
    forward(1, 0)
    attend_heads(16, 16, 1)
    for load in loads[3:]:
        load.wait()
    for copy in weight_copies:
        copy.wait_recv()
    project(0, 0)
    forward(1, 1)
    forward(1, 3)
    project(0, 1)
    project(0, 3)
    sent(1)
    forward(1, 2)
    project(0, 2)
    activate(0)
    for kc in (1, 3, 2, 0):
        give_back(0, kc)
    for kc in (0, 1, 3, 2):
        project(1, kc)
    activate(1)
    for kb in (1, 3, 2, 0):
        back(0, kb)
    for kc in (1, 3, 2, 0):
        give_back(1, kc)
    combine(0, 0)
    combine(0, 1)
    combine(0, 3)
    for kb in (1, 3, 2, 0):
        back(1, kb)
    combine(0, 2)
    for kb in (0, 1, 3, 2):
        combine(1, kb)

    back3 = {}
    for s, (start, width) in enumerate(SLICES):
        for k in NEAR_FIRST:
            gs[s][k] = part[k * TOK:(k + 1) * TOK, start:start + width].astype(BF16)
            copy = remote(
                gs[s].at[k], fins[s].at[k], r3send.at[s, k], r3recv.at[s, k],
                peer(ORDERS[s][0], -k),
            )
            copy.start()
            back3[s, k] = copy
    for s, (start, width) in enumerate(SLICES):
        total = part[0:TOK, start:start + width]
        for k in (1, 3, 2):
            back3[s, k].wait_recv()
            total = total + fins[s][k].astype(F32)
        mix_ref[:, start:start + width] = total.astype(BF16)

    kv_copy.wait_send()
    for copies in (table_copies, weight_copies, hop1.values(), back1.values(), back2.values(),
                   back3.values()):
        for copy in copies:
            copy.wait_send()


def experts_and_attention(
    hidden, again, egain, routes, rweight, lengths, queries, kproj, vproj, gate, up, down
):
    vmem = pl.BlockSpec(memory_space=pltpu.VMEM)
    smem = pl.BlockSpec(memory_space=pltpu.SMEM)
    hbm = pl.BlockSpec(memory_space=pl.ANY)
    dma = pltpu.SemaphoreType.DMA
    widths = [width for _, width in SLICES]
    scratch = [
        pltpu.VMEM((D, 2 * FE), BF16),
        pltpu.VMEM((FE, D), BF16),
        pltpu.VMEM((64, PARTS[0][1], 2 * FE), F32),
        pltpu.VMEM((64, PARTS[1][1], 2 * FE), F32),
        pltpu.VMEM((LINE * TOK, D), F32),
        pltpu.VMEM((TOK, HQ * HD), BF16),
        pltpu.VMEM((D, KVH * HD), BF16),
        pltpu.VMEM((D, KVH * HD), BF16),
        pltpu.VMEM((2, TOK, 2 * KVH * HD), BF16),
        pltpu.VMEM((10, 2, 64, TOK), F32),
    ]
    scratch += [pltpu.VMEM((4, TOK, w), BF16) for w in widths]
    scratch += [pltpu.VMEM((4, TOK, w), BF16) for w in widths]
    for _ in range(3):
        for _, count in PARTS:
            scratch += [pltpu.VMEM((4, 4, LINE * count, w), BF16) for w in widths]
    scratch += [
        dma((6,)), dma((3,)), dma((3,)), dma, dma, dma((10,)), dma((10,)),
        dma((3, 4)), dma((3, 4)), dma((2, 3, 4)), dma((2, 3, 4)),
        dma((2, 3, 4, 4)), dma((2, 3, 4, 4)), dma((2, 3, 4, 4)), dma((2, 3, 4, 4)),
        dma((2, 3, 4)), dma((2, 3, 4)), dma((3, 4)), dma((3, 4)),
        pltpu.SemaphoreType.REGULAR((2, 3, 4)),
    ]
    return pl.pallas_call(
        expert_kernel,
        out_shape=(
            jax.ShapeDtypeStruct((TOK, HQ * HD), BF16),
            jax.ShapeDtypeStruct((TOK, D), BF16),
        ),
        in_specs=[vmem, vmem, vmem, vmem, vmem, smem] + [hbm] * 6,
        out_specs=(vmem, vmem),
        scratch_shapes=scratch,
        compiler_params=pltpu.CompilerParams(
            collective_id=1, has_side_effects=True, vmem_limit_bytes=62 << 20
        ),
        name="experts_and_attention",
    )(hidden, again, egain, routes, rweight, lengths, queries, kproj, vproj, gate, up, down)


DV = 1152
FH = 1152
N_WIDE = 64


def vision_kernel(
    patches_ref, gain_ref, spots_ref, text_ref, up_hbm, down_hbm, merger_hbm,
    hidden_ref,
    up, down, merger, ordered, own, psend, precv, half_send, half_recv, rows_f, rows, arrived,
    arrived_f, spots,
    local_sem, psend_sem, precv_sem, hsend_sem, hrecv_sem, ssend, srecv, rsend, rrecv,
):
    wide = lax.axis_index("wide")
    narrow = lax.axis_index("narrow")
    place = (wide // 16, lax.rem(wide // 4, 4), lax.rem(wide, 4))
    partner = (wide, 1 - narrow)

    def peer(axis, step):
        return (wide_of(shifted(place, axis, step)), narrow)

    def offset_wide(k):
        return wide_of(
            shifted(shifted(shifted(place, 0, k // 16), 1, lax.rem(k // 4, 4)), 2, lax.rem(k, 4))
        )

    def remote(src, dst, send, recv, device):
        return pltpu.make_async_remote_copy(
            src_ref=src, dst_ref=dst, send_sem=send, recv_sem=recv, device_id=device,
            device_id_type=MESH,
        )

    loads = [
        pltpu.make_async_copy(up_hbm, up, local_sem.at[0]),
        pltpu.make_async_copy(down_hbm, down, local_sem.at[1]),
        pltpu.make_async_copy(merger_hbm, merger, local_sem.at[2]),
    ]
    for load in loads:
        load.start()
    barrier = pltpu.get_barrier_semaphore()
    pl.semaphore_signal(barrier, inc=1, device_id=partner, device_id_type=MESH)

    def greet(k, carry):
        pl.semaphore_signal(
            barrier, inc=1, device_id=(offset_wide(k), narrow), device_id_type=MESH
        )
        return carry

    lax.fori_loop(1, N_WIDE, greet, 0)

    row = lane_iota((4 * TOK, 4 * TOK), 0)
    order = (lane_iota((4 * TOK, 4 * TOK), 1) == 4 * lax.rem(row, TOK) + row // TOK)
    order = jnp.where(order, 1.0, 0.0).astype(BF16)
    ordered[...] = jnp.dot(order, patches_ref[...], preferred_element_type=F32)
    spots[0, 0, 0] = jnp.broadcast_to(spots_ref[...], (8, TOK)).astype(F32)

    def spot_hop(axis):
        copies = []
        for k in (2, 1, 3):
            if axis == 0:
                src, dst = spots.at[0, 0, 0], spots.at[k, 0, 0]
            elif axis == 1:
                src, dst = spots.at[:, 0, 0], spots.at[:, k, 0]
            else:
                src, dst = spots.at[:, :, 0], spots.at[:, :, k]
            copy = remote(src, dst, ssend.at[axis, k], srecv.at[axis, k], peer(axis, k))
            copy.start()
            copies.append(copy)
        return copies

    halves = []
    spot_copies = []
    for m in range(MERGE):
        patch = ordered[m * TOK:(m + 1) * TOK]
        mean = jnp.mean(patch, axis=-1, keepdims=True)
        centered = patch - mean
        variance = jnp.mean(centered * centered, axis=-1, keepdims=True)
        normed = (centered * lax.rsqrt(variance + EPSILON) * gain_ref[...]).astype(BF16)
        if m == 0:
            loads[0].wait()
        inner = jnp.dot(normed, up[...], preferred_element_type=F32)
        inner = jax.nn.gelu(inner, approximate=True).astype(BF16)
        if m == 0:
            loads[1].wait()
        partial = jnp.dot(inner, down[...], preferred_element_type=F32)
        own[m] = patch + partial
        psend[m] = partial.astype(BF16)
        if m == 0:
            pl.semaphore_wait(barrier, N_WIDE)
        copy = remote(psend.at[m], precv.at[m], psend_sem.at[m], precv_sem.at[m], partner)
        copy.start()
        halves.append(copy)
        if m == 0:
            spot_copies += spot_hop(0)
    for copy in spot_copies:
        copy.wait_recv()
    spot_copies += spot_hop(1)

    loads[2].wait()
    visual = jnp.zeros((TOK, D // 2), F32)
    for m in range(MERGE):
        halves[m].wait_recv()
        merged = (own[m] + precv[m].astype(F32)).astype(BF16)
        visual = visual + jnp.dot(
            merged, merger[m * DV:(m + 1) * DV], preferred_element_type=F32
        )
    visual = visual.astype(BF16)

    row = lane_iota((TOK, TOK), 0)
    wanted = 2 * lax.rem(row, N_WIDE) + jnp.where(row < N_WIDE, narrow, 1 - narrow)
    choose = jnp.where(lane_iota((TOK, TOK), 1) == wanted, 1.0, 0.0).astype(BF16)
    sorted_rows = jnp.dot(choose, visual, preferred_element_type=F32)
    half_send[...] = sorted_rows[N_WIDE:].astype(BF16)
    half_copy = remote(half_send, half_recv, hsend_sem, hrecv_sem, partner)
    half_copy.start()
    for j in range(8):
        rows_f[:, narrow, j, :] = sorted_rows[:N_WIDE, j * TOK:(j + 1) * TOK]
    half_copy.wait_recv()
    other = half_recv[...].astype(F32)
    for j in range(8):
        rows_f[:, 1 - narrow, j, :] = other[:, j * TOK:(j + 1) * TOK]
    rows[...] = rows_f[...].reshape(N_WIDE, 16, TOK).astype(BF16)

    def row_copy(k):
        target = offset_wide(k)
        return remote(rows.at[target], arrived.at[k], rsend.at[k], rrecv.at[k], (target, narrow))

    def start_row(k, carry):
        row_copy(k).start()
        return carry

    def wait_row(k, carry):
        row_copy(k).wait()
        return carry

    lax.fori_loop(1, N_WIDE, start_row, 0, unroll=7)
    for copy in spot_copies[3:6]:
        copy.wait_recv()
    spot_copies += spot_hop(2)
    arrived[0] = rows[wide]
    for copy in spot_copies[6:]:
        copy.wait_recv()
    spot_rows = spots[...].reshape(N_WIDE, 8, TOK)[:, 0, :]
    lane = lane_iota((N_WIDE, TOK), 1)
    spot = jnp.sum(jnp.where(lane == 2 * wide + narrow, spot_rows, 0.0), axis=1, keepdims=True)
    put = jnp.where(lane.astype(F32) == spot, 1.0, 0.0).astype(BF16)
    flag = lax.dot_general(
        put, jnp.ones((N_WIDE, TOK), BF16), (((0,), (0,)), ((), ())), preferred_element_type=F32
    )[:, 0:1]
    lax.fori_loop(1, N_WIDE, wait_row, 0, unroll=7)
    arrived_f[...] = arrived[...].astype(F32)
    columns = jnp.concatenate([arrived_f[:, j, :] for j in range(16)], axis=1).astype(BF16)
    placed = lax.dot_general(put, columns, (((0,), (0,)), ((), ())), preferred_element_type=F32)
    hidden_ref[...] = jnp.where(flag > 0.5, placed, text_ref[...].astype(F32)).astype(BF16)

    half_copy.wait_send()
    for copies in (halves, spot_copies):
        for copy in copies:
            copy.wait_send()


def vision_and_placement(patches, gain, spots, text, up, down, merger):
    vmem = pl.BlockSpec(memory_space=pltpu.VMEM)
    hbm = pl.BlockSpec(memory_space=pl.ANY)
    dma = pltpu.SemaphoreType.DMA
    return pl.pallas_call(
        vision_kernel,
        out_shape=jax.ShapeDtypeStruct((TOK, D), BF16),
        in_specs=[vmem] * 4 + [hbm] * 3,
        out_specs=vmem,
        scratch_shapes=[
            pltpu.VMEM((DV, FH), BF16),
            pltpu.VMEM((FH, DV), BF16),
            pltpu.VMEM((MERGE * DV, D // 2), BF16),
            pltpu.VMEM((MERGE * TOK, DV), F32),
            pltpu.VMEM((MERGE, TOK, DV), F32),
            pltpu.VMEM((MERGE, TOK, DV), BF16),
            pltpu.VMEM((MERGE, TOK, DV), BF16),
            pltpu.VMEM((N_WIDE, D // 2), BF16),
            pltpu.VMEM((N_WIDE, D // 2), BF16),
            pltpu.VMEM((N_WIDE, 2, 8, TOK), F32),
            pltpu.VMEM((N_WIDE, 16, TOK), BF16),
            pltpu.VMEM((N_WIDE, 16, TOK), BF16),
            pltpu.VMEM((N_WIDE, 16, TOK), F32),
            pltpu.VMEM((4, 4, 4, 8, TOK), F32),
            dma((3,)), dma((4,)), dma((4,)), dma, dma, dma((3, 4)), dma((3, 4)),
            dma((N_WIDE,)), dma((N_WIDE,)),
        ],
        compiler_params=pltpu.CompilerParams(
            collective_id=0, has_side_effects=True, vmem_limit_bytes=56 << 20
        ),
        name="vision_and_placement",
    )(patches, gain, spots, text, up, down, merger)


def local(
    patches,
    vision_gain,
    vision_up,
    vision_down,
    merger,
    visual_spots,
    text_embed,
    queries,
    attention_gain,
    key_proj,
    value_proj,
    prompt_lengths,
    expert_gain,
    routes,
    route_weight,
    gate_weight,
    up_weight,
    down_weight,
):
    hidden = vision_and_placement(
        patches, vision_gain.reshape(1, -1), visual_spots.reshape(1, -1), text_embed, vision_up,
        vision_down, merger,
    )
    return experts_and_attention(
        hidden, attention_gain.reshape(1, -1), expert_gain.reshape(1, -1), routes.T, route_weight.T,
        prompt_lengths, queries, key_proj, value_proj, gate_weight, up_weight, down_weight,
    )


def solution(mesh):
    return jax.shard_map(
        local,
        mesh=mesh,
        in_specs=(
            P("wide", None),
            P(),
            P(None, "narrow"),
            P("narrow", None),
            P(None, "narrow"),
            P("wide"),
            P(("wide", "narrow"), None),
            P(("wide", "narrow"), None),
            P(),
            P(),
            P(),
            P("wide"),
            P(),
            P(("wide", "narrow"), None),
            P(("wide", "narrow"), None),
            P("wide", None, "narrow"),
            P("wide", None, "narrow"),
            P("wide", "narrow", None),
        ),
        out_specs=(P(("wide", "narrow"), None), P(("wide", "narrow"), None)),
        check_vma=False,
    )
```

```python
import functools

import jax
import jax.numpy as jnp
from jax import lax
from jax.experimental import pallas as pl
from jax.experimental.pallas import tpu as pltpu
from jax.sharding import PartitionSpec as P

MERGE = 4
HQ = 32
KVH = 2
HD = 128
D = 2048
DV = 1152
FH = 1152
N_WIDE = 64
FE = 768
HALF = FE // 2
CAP = 24
TOK = 128
LINE = 4
PARTS = ((0, 16), (16, 8))
EPSILON = 1e-06
MESH = pl.DeviceIdType.MESH
BF16 = jnp.bfloat16
F32 = jnp.float32

SLICES = ((0, 640), (640, 640), (1280, 768))
ORDERS = ((0, 1, 2), (1, 2, 0), (2, 0, 1))
NEAR_FIRST = (1, 3, 2)


def wide_of(place):
    return place[0] * 16 + place[1] * 4 + place[2]


def shifted(place, axis, step):
    moved = list(place)
    moved[axis] = lax.rem(place[axis] + step + 4, 4)
    return tuple(moved)


def source_index(order, ka, kb, kc):
    offset = [0, 0, 0]
    offset[order[0]], offset[order[1]], offset[order[2]] = ka, kb, kc
    return offset[0] * 16 + offset[1] * 4 + offset[2]


def lane_iota(shape, dim):
    return lax.broadcasted_iota(jnp.int32, shape, dim)


def layer_kernel(
    patches_ref, gain_ref, spots_ref, text_ref, again_ref, egain_ref, routes_ref, rweight_ref,
    length_ref, vup_hbm, vdown_hbm, merger_hbm, queries_hbm, kproj_hbm, vproj_hbm, gate_hbm, up_hbm,
    down_hbm,
    attended_ref, mix_ref,
    gu, dn, queries, kproj, vproj, kv, tables, precv, half_recv, arrived, spots,
    g0, g1, g2, fin0, fin1, fin2,
    tx00, tx01, tx02, tx10, tx11, tx12, mid00, mid01, mid02, mid10, mid11, mid12,
    rx00, rx01, rx02, rx10, rx11, rx12,
    local_sem, wsend, wrecv, kvsend, kvrecv, tsend, trecv,
    s1send, s1recv, s2send, s2recv, s3send, s3recv,
    r1send, r1recv, r2send, r2recv, r3send, r3recv, free_sem,
    psend_sem, precv_sem, hsend_sem, hrecv_sem, ssend, srecv, rsend, rrecv,
):
    gs, fins = (g0, g1, g2), (fin0, fin1, fin2)
    txs = ((tx00, tx01, tx02), (tx10, tx11, tx12))
    mids = ((mid00, mid01, mid02), (mid10, mid11, mid12))
    rxs = ((rx00, rx01, rx02), (rx10, rx11, rx12))
    wide = lax.axis_index("wide")
    narrow = lax.axis_index("narrow")
    place = (wide // 16, lax.rem(wide // 4, 4), lax.rem(wide, 4))
    partner = (wide, 1 - narrow)

    def peer(axis, step):
        return (wide_of(shifted(place, axis, step)), narrow)

    def offset_wide(k):
        return wide_of(
            shifted(shifted(shifted(place, 0, k // 16), 1, lax.rem(k // 4, 4)), 2, lax.rem(k, 4))
        )

    def remote(src, dst, send, recv, device):
        return pltpu.make_async_remote_copy(
            src_ref=src, dst_ref=dst, send_sem=send, recv_sem=recv, device_id=device,
            device_id_type=MESH,
        )

    barrier = pltpu.get_barrier_semaphore()
    pl.semaphore_signal(barrier, inc=1, device_id=partner, device_id_type=MESH)

    def greet(k, carry):
        pl.semaphore_signal(
            barrier, inc=1, device_id=(offset_wide(k), narrow), device_id_type=MESH
        )
        return carry

    lax.fori_loop(1, N_WIDE, greet, 0)

    loads = [
        pltpu.make_async_copy(kproj_hbm, kproj, local_sem.at[0]),
        pltpu.make_async_copy(vproj_hbm, vproj, local_sem.at[1]),
        pltpu.make_async_copy(queries_hbm, queries, local_sem.at[2]),
        pltpu.make_async_copy(gate_hbm.at[0], gu.at[:, 0:HALF], local_sem.at[3]),
        pltpu.make_async_copy(up_hbm.at[0], gu.at[:, FE:FE + HALF], local_sem.at[4]),
        pltpu.make_async_copy(down_hbm.at[0], dn.at[0:HALF, :], local_sem.at[5]),
    ]
    hop1 = {}
    table_copies = []
    for axis in range(3):
        for step in (1, 2, 3):
            slot = 1 + axis * 3 + step - 1
            table_copies.append(
                remote(
                    tables.at[0], tables.at[slot], tsend.at[slot], trecv.at[slot],
                    peer(axis, step),
                )
            )
    for s in range(3):
        for k in (1, 2, 3):
            hop1[s, k] = remote(
                gs[s].at[0], gs[s].at[k], s1send.at[s, k], s1recv.at[s, k],
                peer(ORDERS[s][0], k),
            )
    kv_copy = remote(kv.at[narrow], kv.at[narrow], kvsend, kvrecv, partner)
    weight_copies = [
        remote(gate_hbm.at[0], gu.at[:, HALF:FE], wsend.at[0], wrecv.at[0], partner),
        remote(up_hbm.at[0], gu.at[:, FE + HALF:], wsend.at[1], wrecv.at[1], partner),
        remote(down_hbm.at[0], dn.at[HALF:, :], wsend.at[2], wrecv.at[2], partner),
    ]

    def send_tables():
        expert_iota = lane_iota((64, TOK), 0)
        member = jnp.zeros((64, TOK), F32)
        weight = jnp.zeros((64, TOK), F32)
        for k in range(8):
            hit = routes_ref[k:k + 1, :] == expert_iota
            member = member + jnp.where(hit, 1.0, 0.0)
            weight = weight + jnp.where(hit, rweight_ref[k:k + 1, :], 0.0)
        before = (lane_iota((TOK, TOK), 0) < lane_iota((TOK, TOK), 1)).astype(F32).astype(BF16)
        rank = jnp.dot(member.astype(BF16), before, preferred_element_type=F32)
        tables[0, 0] = jnp.where(member > 0.5, rank, -1.0)
        tables[0, 1] = weight

        for copy in table_copies:
            copy.start()

    def send_weights():
        for copy in weight_copies:
            copy.start()

    def vision(up, down, merger, ordered, own, psend, half_send, rows_f, rows, arrived_f):
        vision_loads = [
            pltpu.make_async_copy(vup_hbm, up, local_sem.at[6]),
            pltpu.make_async_copy(vdown_hbm, down, local_sem.at[7]),
        ]
        merger_loads = [
            pltpu.make_async_copy(
                merger_hbm.at[pl.ds(m * DV, DV)], merger.at[m % 2], local_sem.at[8 + m]
            )
            for m in range(MERGE)
        ]
        for load in vision_loads + merger_loads[:2] + loads:
            load.start()
        row = lane_iota((4 * TOK, 4 * TOK), 0)
        order = (lane_iota((4 * TOK, 4 * TOK), 1) == 4 * lax.rem(row, TOK) + row // TOK)
        order = jnp.where(order, 1.0, 0.0).astype(BF16)
        ordered[...] = jnp.dot(order, patches_ref[...], preferred_element_type=F32).astype(BF16)
        spots[0, 0, 0] = jnp.broadcast_to(spots_ref[...], (8, TOK)).astype(F32)

        def spot_hop(axis):
            copies = []
            for k in (2, 1, 3):
                if axis == 0:
                    src, dst = spots.at[0, 0, 0], spots.at[k, 0, 0]
                elif axis == 1:
                    src, dst = spots.at[:, 0, 0], spots.at[:, k, 0]
                else:
                    src, dst = spots.at[:, :, 0], spots.at[:, :, k]
                copy = remote(src, dst, ssend.at[axis, k], srecv.at[axis, k], peer(axis, k))
                copy.start()
                copies.append(copy)
            return copies

        halves = []
        spot_copies = []
        for m in range(MERGE):
            patch = ordered[m * TOK:(m + 1) * TOK].astype(F32)
            mean = jnp.mean(patch, axis=-1, keepdims=True)
            centered = patch - mean
            variance = jnp.mean(centered * centered, axis=-1, keepdims=True)
            normed = (centered * lax.rsqrt(variance + EPSILON) * gain_ref[...].reshape(1, DV)).astype(BF16)
            if m == 0:
                vision_loads[0].wait()
            inner = jnp.dot(normed, up[...], preferred_element_type=F32)
            inner = jax.nn.gelu(inner, approximate=True).astype(BF16)
            if m == 0:
                vision_loads[1].wait()
            partial = jnp.dot(inner, down[...], preferred_element_type=F32)
            own[m] = patch + partial
            psend[m] = partial.astype(BF16)
            if m == 0:
                pl.semaphore_wait(barrier, N_WIDE)
            copy = remote(psend.at[m], precv.at[m], psend_sem.at[m], precv_sem.at[m], partner)
            copy.start()
            halves.append(copy)
            if m == 0:
                spot_copies += spot_hop(0)
                send_tables()
        for copy in spot_copies:
            copy.wait_recv()
        spot_copies += spot_hop(1)

        send_weights()
        visual = jnp.zeros((TOK, D // 2), F32)
        for m in range(MERGE):
            halves[m].wait_recv()
            merger_loads[m].wait()
            merged = (own[m] + precv[m].astype(F32)).astype(BF16)
            visual = visual + jnp.dot(
                merged, merger[m % 2], preferred_element_type=F32
            )
            if m + 2 < MERGE:
                merger_loads[m + 2].start()
        visual = visual.astype(BF16)

        row = lane_iota((TOK, TOK), 0)
        wanted = 2 * lax.rem(row, N_WIDE) + jnp.where(row < N_WIDE, narrow, 1 - narrow)
        choose = jnp.where(lane_iota((TOK, TOK), 1) == wanted, 1.0, 0.0).astype(BF16)
        sorted_rows = jnp.dot(choose, visual, preferred_element_type=F32)
        half_send[...] = sorted_rows[N_WIDE:].astype(BF16)
        half_copy = remote(half_send, half_recv, hsend_sem, hrecv_sem, partner)
        half_copy.start()
        for j in range(8):
            rows_f[:, narrow, j, :] = sorted_rows[:N_WIDE, j * TOK:(j + 1) * TOK]
        half_copy.wait_recv()
        other = half_recv[...].astype(F32)
        for j in range(8):
            rows_f[:, 1 - narrow, j, :] = other[:, j * TOK:(j + 1) * TOK]
        rows[...] = rows_f[...].reshape(N_WIDE, 16, TOK).astype(BF16)

        def row_copy(k):
            target = offset_wide(k)
            return remote(rows.at[target], arrived.at[k], rsend.at[k], rrecv.at[k], (target, narrow))

        def start_row(k, carry):
            row_copy(k).start()
            return carry

        def wait_row(k, carry):
            row_copy(k).wait()
            return carry

        lax.fori_loop(1, N_WIDE, start_row, 0, unroll=7)
        for copy in spot_copies[3:6]:
            copy.wait_recv()
        spot_copies += spot_hop(2)
        arrived[0] = rows[wide]
        for copy in spot_copies[6:]:
            copy.wait_recv()
        spot_rows = spots[...].reshape(N_WIDE, 8, TOK)[:, 0, :]
        lane = lane_iota((N_WIDE, TOK), 1)
        spot = jnp.sum(jnp.where(lane == 2 * wide + narrow, spot_rows, 0.0), axis=1, keepdims=True)
        put = jnp.where(lane.astype(F32) == spot, 1.0, 0.0).astype(BF16)
        flag = lax.dot_general(
            put, jnp.ones((N_WIDE, TOK), BF16), (((0,), (0,)), ((), ())), preferred_element_type=F32
        )[:, 0:1]
        lax.fori_loop(1, N_WIDE, wait_row, 0, unroll=7)
        arrived_f[...] = arrived[...].astype(F32)
        columns = jnp.concatenate([arrived_f[:, j, :] for j in range(16)], axis=1).astype(BF16)
        placed = lax.dot_general(put, columns, (((0,), (0,)), ((), ())), preferred_element_type=F32)
        hidden = jnp.where(flag > 0.5, placed, text_ref[...].astype(F32))
        scale = lax.rsqrt(jnp.mean(hidden * hidden, axis=-1, keepdims=True) + EPSILON)
        scaled = hidden * scale
        moe_in = (scaled * egain_ref[...]).astype(BF16)
        attn_in = (scaled * again_ref[...]).astype(BF16)
        for s, (start, width) in enumerate(SLICES):
            gs[s][0] = moe_in[:, start:start + width]
        for k in NEAR_FIRST:
            for s in range(3):
                hop1[s, k].start()
        loads[0].wait()
        loads[1].wait()
        own_keys = jnp.dot(attn_in, kproj[...], preferred_element_type=F32).astype(BF16)
        own_values = jnp.dot(attn_in, vproj[...], preferred_element_type=F32).astype(BF16)
        kv[narrow, :, 0:KVH * HD] = own_keys
        kv[narrow, :, KVH * HD:] = own_values
        kv_copy.start()

        half_copy.wait_send()
        for copies in (halves, spot_copies):
            for copy in copies:
                copy.wait_send()

    pl.run_scoped(
        vision,
        pltpu.VMEM((DV, FH), BF16),
        pltpu.VMEM((FH, DV), BF16),
        pltpu.VMEM((2, DV, D // 2), BF16),
        pltpu.VMEM((MERGE * TOK, DV), BF16),
        pltpu.VMEM((MERGE, TOK, DV), F32),
        pltpu.VMEM((MERGE, TOK, DV), BF16),
        pltpu.VMEM((N_WIDE, D // 2), BF16),
        pltpu.VMEM((N_WIDE, 2, 8, TOK), F32),
        pltpu.VMEM((N_WIDE, 16, TOK), BF16),
        pltpu.VMEM((N_WIDE, 16, TOK), F32),
    )

    def experts(acc0, acc1, part):
        accs = (acc0, acc1)

        def slot_blocks(p, s, kb, weighted):
            axis_a, axis_b, axis_c = ORDERS[s]
            first, count = PARTS[p]
            slot_iota = lane_iota((LINE * count, LINE * TOK), 0).astype(F32)
            blocks = []
            for kc in range(4):
                expert = wide_of(shifted(shifted(place, axis_b, kb), axis_c, kc))
                rows = []
                weights = []
                for ka in range(4):
                    slot = 0 if ka == 0 else 1 + axis_a * 3 + ka - 1
                    row = tables[slot, 0, pl.ds(expert, 1), :]
                    inside = (row >= float(first)) & (row < float(first + count))
                    rows.append(jnp.where(inside, row + float(count * ka - first), -1.0))
                    if weighted:
                        weights.append(tables[slot, 1, pl.ds(expert, 1), :])
                hit = slot_iota == jnp.concatenate(rows, axis=1)
                if weighted:
                    value = jnp.where(hit, jnp.concatenate(weights, axis=1), 0.0)
                else:
                    value = jnp.where(hit, 1.0, 0.0)
                blocks.append(value.astype(BF16))
            return jnp.concatenate(blocks, axis=0)

        for copy in table_copies:
            copy.wait_recv()

        hop2 = {}

        def build(p, kb):
            for s, (start, width) in enumerate(SLICES):
                tokens = gs[s][...].reshape(LINE * TOK, width)
                rows = jnp.dot(slot_blocks(p, s, kb, False), tokens, preferred_element_type=F32)
                rows = rows.astype(BF16).reshape(4, LINE * PARTS[p][1], width)
                if kb == 0:
                    mids[p][s][0] = rows
                else:
                    txs[p][s][kb] = rows
                    copy = remote(
                        txs[p][s].at[kb], mids[p][s].at[kb], s2send.at[p, s, kb],
                        s2recv.at[p, s, kb], peer(ORDERS[s][1], kb),
                    )
                    copy.start()
                    hop2[p, s, kb] = copy

        hop3 = {}

        def forward(p, kb):
            for s in range(3):
                if kb:
                    hop2[p, s, kb].wait_recv()
                for kc in NEAR_FIRST:
                    copy = remote(
                        mids[p][s].at[kb, kc], rxs[p][s].at[kc, kb], s3send.at[p, s, kc, kb],
                        s3recv.at[p, s, kc, kb], peer(ORDERS[s][2], kc),
                    )
                    copy.start()
                    hop3[p, s, kc, kb] = copy

        def sent(p):
            for (part_of, _, _), copy in hop2.items():
                if part_of == p:
                    copy.wait_send()

        def attend(head, group, allowed):
            columns = pl.ds(pl.multiple_of(head * HD, HD), HD)
            keys = kv[:, :, group * HD:(group + 1) * HD].reshape(2 * TOK, HD)
            values = kv[:, :, (KVH + group) * HD:(KVH + group + 1) * HD].reshape(2 * TOK, HD)
            scores = lax.dot_general(
                queries[:, columns], keys, (((1,), (1,)), ((), ())), preferred_element_type=F32
            ) * HD ** (-0.5)
            scores = jnp.where(allowed, scores, -1e30)
            row_max = jnp.max(scores, axis=-1, keepdims=True)
            weights = jnp.exp(scores - row_max)
            total = jnp.sum(weights, axis=-1, keepdims=True)
            mixed = jnp.dot(weights.astype(BF16), values, preferred_element_type=F32)
            attended_ref[:, columns] = (mixed / total).astype(BF16)

        def attend_heads(first, count, group):
            row_pos = lane_iota((TOK, 2 * TOK), 0) + narrow * TOK
            key_pos = lane_iota((TOK, 2 * TOK), 1)
            allowed = key_pos <= jnp.minimum(row_pos, length_ref[0] - 1)

            def body(i, carry):
                for j in range(4):
                    attend(first + i * 4 + j, group, allowed)
                return carry
            lax.fori_loop(0, count // 4, body, 0)

        written = set()

        def project(p, kc):
            count = PARTS[p][1]
            for s, (start, width) in enumerate(SLICES):
                if kc:
                    for kb in range(4):
                        hop3[p, s, kc, kb].wait_recv()
                    rows = rxs[p][s][kc].reshape(16 * count, width)
                else:
                    rows = mids[p][s][:, 0].reshape(16 * count, width)
                for n in range(2):
                    out = jnp.dot(
                        rows, gu[start:start + width, n * FE:(n + 1) * FE], preferred_element_type=F32
                    ).reshape(4, 4, count, FE)
                    for kb in range(4):
                        for ka in range(4):
                            index = source_index(ORDERS[s], ka, kb, kc)
                            if (p, n, index) in written:
                                accs[p][index, :, n * FE:(n + 1) * FE] += out[kb, ka]
                            else:
                                written.add((p, n, index))
                                accs[p][index, :, n * FE:(n + 1) * FE] = out[kb, ka]

        def activate(p):
            acc = accs[p]

            def body(i, carry):
                gate = acc[i, :, 0:FE]
                up = acc[i, :, FE:]
                acc[i, :, 0:FE] = gate * (1.0 / (1.0 + jnp.exp(-gate))) * up
                return carry

            lax.fori_loop(0, 64, body, 0)
            for (part_of, _, _, _), copy in hop3.items():
                if part_of == p:
                    copy.wait_send()
            for s in range(3):
                for kb in (1, 2, 3):
                    pl.semaphore_signal(
                        free_sem.at[p, s, kb], inc=1, device_id=peer(ORDERS[s][1], kb),
                        device_id_type=MESH,
                    )

        back1 = {}

        def give_back(p, kc):
            count = PARTS[p][1]
            for s, (start, width) in enumerate(SLICES):
                pieces = [
                    accs[p][source_index(ORDERS[s], ka, kb, kc), :, 0:FE]
                    for kb in range(4) for ka in range(4)
                ]
                active = jnp.concatenate(pieces, axis=0).astype(BF16)
                out = jnp.dot(active, dn[:, start:start + width], preferred_element_type=F32)
                out = out.astype(BF16).reshape(4, LINE * count, width)
                if kc == 0:
                    txs[p][s][:, 0] = out
                else:
                    rxs[p][s][kc] = out
                    for kb in (1, 3, 2, 0):
                        copy = remote(
                            rxs[p][s].at[kc, kb], txs[p][s].at[kb, kc], r1send.at[p, s, kc, kb],
                            r1recv.at[p, s, kc, kb], peer(ORDERS[s][2], -kc),
                        )
                        copy.start()
                        back1[p, s, kc, kb] = copy

        back2 = {}

        def back(p, kb):
            for s in range(3):
                for kc in NEAR_FIRST:
                    back1[p, s, kc, kb].wait_recv()
                if kb:
                    pl.semaphore_wait(free_sem.at[p, s, kb], 1)
                    copy = remote(
                        txs[p][s].at[kb], mids[p][s].at[kb], r2send.at[p, s, kb],
                        r2recv.at[p, s, kb], peer(ORDERS[s][1], -kb),
                    )
                    copy.start()
                    back2[p, s, kb] = copy

        def combine(p, kb, s):
            start, width = SLICES[s]
            if kb:
                back2[p, s, kb].wait_recv()
                rows = mids[p][s][kb].reshape(16 * PARTS[p][1], width)
            else:
                rows = txs[p][s][0].reshape(16 * PARTS[p][1], width)
            total = lax.dot_general(
                slot_blocks(p, s, kb, True), rows, (((0,), (0,)), ((), ())),
                preferred_element_type=F32,
            )
            if p or kb:
                part[:, start:start + width] += total
            else:
                part[:, start:start + width] = total

        for s in range(3):
            for k in (1, 2, 3):
                hop1[s, k].wait_recv()
        for kb in (1, 3, 2, 0):
            build(0, kb)
        forward(0, 0)
        kv_copy.wait_recv()
        loads[2].wait()
        attend_heads(0, 16, 0)
        forward(0, 1)
        forward(0, 3)
        for kb in (1, 3, 2, 0):
            build(1, kb)
        sent(0)
        forward(0, 2)
        forward(1, 0)
        attend_heads(16, 16, 1)
        for load in loads[3:]:
            load.wait()
        for copy in weight_copies:
            copy.wait_recv()
        project(0, 0)
        forward(1, 1)
        forward(1, 3)
        project(0, 1)
        project(0, 3)
        sent(1)
        forward(1, 2)
        project(0, 2)
        activate(0)
        for kc in (1, 3, 2, 0):
            give_back(0, kc)
        for kc in (0, 1, 3, 2):
            project(1, kc)
        activate(1)
        back(0, 1)
        back(0, 3)
        for kc in (1, 3, 2, 0):
            give_back(1, kc)
        back(0, 2)
        back(0, 0)
        for s in range(3):
            combine(0, 0, s)
        for kb in (1, 3, 2, 0):
            back(1, kb)
        for kb in (1, 3, 2):
            for s in range(3):
                combine(0, kb, s)

        back3 = {}
        for s, (start, width) in enumerate(SLICES):
            for kb in (0, 1, 3, 2):
                combine(1, kb, s)
            for k in (2, 1, 3):
                gs[s][k] = part[k * TOK:(k + 1) * TOK, start:start + width].astype(BF16)
                copy = remote(
                    gs[s].at[k], fins[s].at[k], r3send.at[s, k], r3recv.at[s, k],
                    peer(ORDERS[s][0], -k),
                )
                copy.start()
                back3[s, k] = copy
        for s, (start, width) in enumerate(SLICES):
            total = part[0:TOK, start:start + width]
            for k in (1, 3, 2):
                back3[s, k].wait_recv()
                total = total + fins[s][k].astype(F32)
            mix_ref[:, start:start + width] = total.astype(BF16)

        kv_copy.wait_send()
        for copies in (table_copies, weight_copies, hop1.values(), back1.values(), back2.values(),
                       back3.values()):
            for copy in copies:
                copy.wait_send()

    pl.run_scoped(
        experts,
        pltpu.VMEM((64, PARTS[0][1], 2 * FE), F32),
        pltpu.VMEM((64, PARTS[1][1], 2 * FE), F32),
        pltpu.VMEM((LINE * TOK, D), F32),
    )


def layer(
    patches, gain, spots, text, again, egain, routes, rweight, lengths, vup, vdown, merger,
    queries, kproj, vproj, gate, up, down,
):
    vmem = pl.BlockSpec(memory_space=pltpu.VMEM)
    smem = pl.BlockSpec(memory_space=pltpu.SMEM)
    hbm = pl.BlockSpec(memory_space=pl.ANY)
    dma = pltpu.SemaphoreType.DMA
    widths = [width for _, width in SLICES]
    scratch = [
        pltpu.VMEM((D, 2 * FE), BF16),
        pltpu.VMEM((FE, D), BF16),
        pltpu.VMEM((TOK, HQ * HD), BF16),
        pltpu.VMEM((D, KVH * HD), BF16),
        pltpu.VMEM((D, KVH * HD), BF16),
        pltpu.VMEM((2, TOK, 2 * KVH * HD), BF16),
        pltpu.VMEM((10, 2, 64, TOK), F32),
        pltpu.VMEM((MERGE, TOK, DV), BF16),
        pltpu.VMEM((N_WIDE, D // 2), BF16),
        pltpu.VMEM((N_WIDE, 16, TOK), BF16),
        pltpu.VMEM((4, 4, 4, 8, TOK), F32),
    ]
    scratch += [pltpu.VMEM((4, TOK, w), BF16) for w in widths]
    scratch += [pltpu.VMEM((4, TOK, w), BF16) for w in widths]
    for _ in range(3):
        for _, count in PARTS:
            scratch += [pltpu.VMEM((4, 4, LINE * count, w), BF16) for w in widths]
    scratch += [
        dma((12,)), dma((3,)), dma((3,)), dma, dma, dma((10,)), dma((10,)),
        dma((3, 4)), dma((3, 4)), dma((2, 3, 4)), dma((2, 3, 4)),
        dma((2, 3, 4, 4)), dma((2, 3, 4, 4)), dma((2, 3, 4, 4)), dma((2, 3, 4, 4)),
        dma((2, 3, 4)), dma((2, 3, 4)), dma((3, 4)), dma((3, 4)),
        pltpu.SemaphoreType.REGULAR((2, 3, 4)),
        dma((4,)), dma((4,)), dma, dma, dma((3, 4)), dma((3, 4)),
        dma((N_WIDE,)), dma((N_WIDE,)),
    ]
    return pl.pallas_call(
        layer_kernel,
        out_shape=(
            jax.ShapeDtypeStruct((TOK, HQ * HD), BF16),
            jax.ShapeDtypeStruct((TOK, D), BF16),
        ),
        in_specs=[vmem] * 8 + [smem] + [hbm] * 9,
        out_specs=(vmem, vmem),
        scratch_shapes=scratch,
        compiler_params=pltpu.CompilerParams(
            collective_id=0, has_side_effects=True, vmem_limit_bytes=64 << 20
        ),
        name="layer",
    )(
        patches, gain, spots, text, again, egain, routes, rweight, lengths, vup, vdown, merger,
        queries, kproj, vproj, gate, up, down,
    )


def local(
    patches,
    vision_gain,
    vision_up,
    vision_down,
    merger,
    visual_spots,
    text_embed,
    queries,
    attention_gain,
    key_proj,
    value_proj,
    prompt_lengths,
    expert_gain,
    routes,
    route_weight,
    gate_weight,
    up_weight,
    down_weight,
):
    return layer(
        patches, vision_gain, visual_spots.reshape(1, -1), text_embed,
        attention_gain.reshape(1, -1), expert_gain.reshape(1, -1), routes.T, route_weight.T,
        prompt_lengths, vision_up, vision_down, merger, queries, key_proj, value_proj, gate_weight,
        up_weight, down_weight,
    )


def solution(mesh):
    return jax.shard_map(
        local,
        mesh=mesh,
        in_specs=(
            P("wide", None),
            P(),
            P(None, "narrow"),
            P("narrow", None),
            P(None, "narrow"),
            P("wide"),
            P(("wide", "narrow"), None),
            P(("wide", "narrow"), None),
            P(),
            P(),
            P(),
            P("wide"),
            P(),
            P(("wide", "narrow"), None),
            P(("wide", "narrow"), None),
            P("wide", None, "narrow"),
            P("wide", None, "narrow"),
            P("wide", "narrow", None),
        ),
        out_specs=(P(("wide", "narrow"), None), P(("wide", "narrow"), None)),
        check_vma=False,
    )
```

```python
import functools

import jax
import jax.numpy as jnp
from jax import lax
from jax.experimental import pallas as pl
from jax.experimental.pallas import tpu as pltpu
from jax.sharding import PartitionSpec as P

MERGE = 4
HQ = 32
KVH = 2
HD = 128
D = 2048
DV = 1152
FH = 1152
N_WIDE = 64
FE = 768
HALF = FE // 2
CAP = 24
TOK = 128
LINE = 4
PARTS = ((0, 16), (16, 8))
EPSILON = 1e-06
MESH = pl.DeviceIdType.MESH
BF16 = jnp.bfloat16
F32 = jnp.float32

SLICES = ((0, 640), (640, 640), (1280, 768))
ORDERS = ((0, 1, 2), (1, 2, 0), (2, 0, 1))
NEAR_FIRST = (1, 3, 2)


def wide_of(place):
    return place[0] * 16 + place[1] * 4 + place[2]


def shifted(place, axis, step):
    moved = list(place)
    moved[axis] = lax.rem(place[axis] + step + 4, 4)
    return tuple(moved)


def source_index(order, ka, kb, kc):
    offset = [0, 0, 0]
    offset[order[0]], offset[order[1]], offset[order[2]] = ka, kb, kc
    return offset[0] * 16 + offset[1] * 4 + offset[2]


def lane_iota(shape, dim):
    return lax.broadcasted_iota(jnp.int32, shape, dim)


def layer_kernel(
    patches_ref, gain_ref, spots_ref, text_ref, again_ref, egain_ref, routes_ref, rweight_ref,
    length_ref, vup_hbm, vdown_hbm, merger_hbm, queries_hbm, kproj_hbm, vproj_hbm, gate_hbm, up_hbm,
    down_hbm,
    attended_ref, mix_ref,
    gu, dn, queries, kproj, vproj, kv, tables, precv, half_recv, arrived, spots,
    g0, g1, g2, fin0, fin1, fin2,
    tx00, tx01, tx02, tx10, tx11, tx12, mid00, mid01, mid02, mid10, mid11, mid12,
    rx00, rx01, rx02, rx10, rx11, rx12,
    local_sem, wsend, wrecv, kvsend, kvrecv, tsend, trecv,
    s1send, s1recv, s2send, s2recv, s3send, s3recv,
    r1send, r1recv, r2send, r2recv, r3send, r3recv, free_sem,
    psend_sem, precv_sem, hsend_sem, hrecv_sem, ssend, srecv, rsend, rrecv,
):
    gs, fins = (g0, g1, g2), (fin0, fin1, fin2)
    txs = ((tx00, tx01, tx02), (tx10, tx11, tx12))
    mids = ((mid00, mid01, mid02), (mid10, mid11, mid12))
    rxs = ((rx00, rx01, rx02), (rx10, rx11, rx12))
    wide = lax.axis_index("wide")
    narrow = lax.axis_index("narrow")
    place = (wide // 16, lax.rem(wide // 4, 4), lax.rem(wide, 4))
    partner = (wide, 1 - narrow)

    def peer(axis, step):
        return (wide_of(shifted(place, axis, step)), narrow)

    def offset_wide(k):
        return wide_of(
            shifted(shifted(shifted(place, 0, k // 16), 1, lax.rem(k // 4, 4)), 2, lax.rem(k, 4))
        )

    def remote(src, dst, send, recv, device):
        return pltpu.make_async_remote_copy(
            src_ref=src, dst_ref=dst, send_sem=send, recv_sem=recv, device_id=device,
            device_id_type=MESH,
        )

    barrier = pltpu.get_barrier_semaphore()
    pl.semaphore_signal(barrier, inc=1, device_id=partner, device_id_type=MESH)

    def greet(k, carry):
        pl.semaphore_signal(
            barrier, inc=1, device_id=(offset_wide(k), narrow), device_id_type=MESH
        )
        return carry


    loads = [
        pltpu.make_async_copy(kproj_hbm, kproj, local_sem.at[0]),
        pltpu.make_async_copy(vproj_hbm, vproj, local_sem.at[1]),
        pltpu.make_async_copy(queries_hbm, queries, local_sem.at[2]),
        pltpu.make_async_copy(gate_hbm.at[0], gu.at[:, 0:HALF], local_sem.at[3]),
        pltpu.make_async_copy(up_hbm.at[0], gu.at[:, FE:FE + HALF], local_sem.at[4]),
        pltpu.make_async_copy(down_hbm.at[0], dn.at[0:HALF, :], local_sem.at[5]),
    ]
    hop1 = {}
    table_copies = []
    for axis in range(3):
        for step in (1, 2, 3):
            slot = 1 + axis * 3 + step - 1
            table_copies.append(
                remote(
                    tables.at[0], tables.at[slot], tsend.at[slot], trecv.at[slot],
                    peer(axis, step),
                )
            )
    for s in range(3):
        for k in (1, 2, 3):
            hop1[s, k] = remote(
                gs[s].at[0], gs[s].at[k], s1send.at[s, k], s1recv.at[s, k],
                peer(ORDERS[s][0], k),
            )
    kv_copy = remote(kv.at[narrow], kv.at[narrow], kvsend, kvrecv, partner)
    weight_copies = [
        remote(gate_hbm.at[0], gu.at[:, HALF:FE], wsend.at[0], wrecv.at[0], partner),
        remote(up_hbm.at[0], gu.at[:, FE + HALF:], wsend.at[1], wrecv.at[1], partner),
        remote(down_hbm.at[0], dn.at[HALF:, :], wsend.at[2], wrecv.at[2], partner),
    ]

    def make_tables():
        expert_iota = lane_iota((64, TOK), 0)
        member = jnp.zeros((64, TOK), F32)
        weight = jnp.zeros((64, TOK), F32)
        for k in range(8):
            hit = routes_ref[k:k + 1, :] == expert_iota
            member = member + jnp.where(hit, 1.0, 0.0)
            weight = weight + jnp.where(hit, rweight_ref[k:k + 1, :], 0.0)
        before = (lane_iota((TOK, TOK), 0) < lane_iota((TOK, TOK), 1)).astype(F32).astype(BF16)
        rank = jnp.dot(member.astype(BF16), before, preferred_element_type=F32)
        tables[0, 0] = jnp.where(member > 0.5, rank, -1.0)
        tables[0, 1] = weight


    def send_tables():
        for copy in table_copies:
            copy.start()

    def send_weights():
        for copy in weight_copies:
            copy.start()

    def vision(up, down, merger, ordered, own, psend, half_send, rows_f, rows, arrived_f):
        vision_loads = [
            pltpu.make_async_copy(vup_hbm, up, local_sem.at[6]),
            pltpu.make_async_copy(vdown_hbm, down, local_sem.at[7]),
        ]
        merger_loads = [
            pltpu.make_async_copy(
                merger_hbm.at[pl.ds(m * DV, DV)], merger.at[m % 2], local_sem.at[8 + m]
            )
            for m in range(MERGE)
        ]
        for load in vision_loads + merger_loads[:2] + loads:
            load.start()
        lax.fori_loop(1, N_WIDE, greet, 0)
        row = lane_iota((4 * TOK, 4 * TOK), 0)
        order = (lane_iota((4 * TOK, 4 * TOK), 1) == 4 * lax.rem(row, TOK) + row // TOK)
        order = jnp.where(order, 1.0, 0.0).astype(BF16)
        ordered[...] = jnp.dot(order, patches_ref[...], preferred_element_type=F32).astype(BF16)
        spots[0, 0, 0] = jnp.broadcast_to(spots_ref[...], (8, TOK)).astype(F32)

        def spot_hop(axis):
            copies = []
            for k in (2, 1, 3):
                if axis == 0:
                    src, dst = spots.at[0, 0, 0], spots.at[k, 0, 0]
                elif axis == 1:
                    src, dst = spots.at[:, 0, 0], spots.at[:, k, 0]
                else:
                    src, dst = spots.at[:, :, 0], spots.at[:, :, k]
                copy = remote(src, dst, ssend.at[axis, k], srecv.at[axis, k], peer(axis, k))
                copy.start()
                copies.append(copy)
            return copies

        halves = []
        spot_copies = []
        for m in range(MERGE):
            patch = ordered[m * TOK:(m + 1) * TOK].astype(F32)
            mean = jnp.mean(patch, axis=-1, keepdims=True)
            centered = patch - mean
            variance = jnp.mean(centered * centered, axis=-1, keepdims=True)
            normed = (centered * lax.rsqrt(variance + EPSILON) * gain_ref[...].reshape(1, DV)).astype(BF16)
            if m == 0:
                vision_loads[0].wait()
            inner = jnp.dot(normed, up[...], preferred_element_type=F32)
            inner = jax.nn.gelu(inner, approximate=True).astype(BF16)
            if m == 0:
                vision_loads[1].wait()
            partial = jnp.dot(inner, down[...], preferred_element_type=F32)
            own[m] = patch + partial
            psend[m] = partial.astype(BF16)
            if m == 0:
                make_tables()
                pl.semaphore_wait(barrier, N_WIDE)
            copy = remote(psend.at[m], precv.at[m], psend_sem.at[m], precv_sem.at[m], partner)
            copy.start()
            halves.append(copy)
            if m == 0:
                spot_copies += spot_hop(0)
                send_tables()
        for copy in spot_copies:
            copy.wait_recv()
        spot_copies += spot_hop(1)

        send_weights()
        visual = jnp.zeros((TOK, D // 2), F32)
        for m in range(MERGE):
            halves[m].wait_recv()
            merger_loads[m].wait()
            merged = (own[m] + precv[m].astype(F32)).astype(BF16)
            visual = visual + jnp.dot(
                merged, merger[m % 2], preferred_element_type=F32
            )
            if m + 2 < MERGE:
                merger_loads[m + 2].start()
        visual = visual.astype(BF16)

        row = lane_iota((TOK, TOK), 0)
        wanted = 2 * lax.rem(row, N_WIDE) + jnp.where(row < N_WIDE, narrow, 1 - narrow)
        choose = jnp.where(lane_iota((TOK, TOK), 1) == wanted, 1.0, 0.0).astype(BF16)
        sorted_rows = jnp.dot(choose, visual, preferred_element_type=F32)
        half_send[...] = sorted_rows[N_WIDE:].astype(BF16)
        half_copy = remote(half_send, half_recv, hsend_sem, hrecv_sem, partner)
        half_copy.start()
        for j in range(8):
            rows_f[:, narrow, j, :] = sorted_rows[:N_WIDE, j * TOK:(j + 1) * TOK]
        half_copy.wait_recv()
        other = half_recv[...].astype(F32)
        for j in range(8):
            rows_f[:, 1 - narrow, j, :] = other[:, j * TOK:(j + 1) * TOK]
        rows[...] = rows_f[...].reshape(N_WIDE, 16, TOK).astype(BF16)

        def row_copy(k):
            target = offset_wide(k)
            return remote(rows.at[target], arrived.at[k], rsend.at[k], rrecv.at[k], (target, narrow))

        def start_row(k, carry):
            row_copy(k).start()
            return carry

        def wait_row(k, carry):
            row_copy(k).wait()
            return carry

        lax.fori_loop(1, N_WIDE, start_row, 0, unroll=7)
        for copy in spot_copies[3:6]:
            copy.wait_recv()
        spot_copies += spot_hop(2)
        arrived[0] = rows[wide]
        for copy in spot_copies[6:]:
            copy.wait_recv()
        spot_rows = spots[...].reshape(N_WIDE, 8, TOK)[:, 0, :]
        lane = lane_iota((N_WIDE, TOK), 1)
        spot = jnp.sum(jnp.where(lane == 2 * wide + narrow, spot_rows, 0.0), axis=1, keepdims=True)
        put = jnp.where(lane.astype(F32) == spot, 1.0, 0.0).astype(BF16)
        flag = lax.dot_general(
            put, jnp.ones((N_WIDE, TOK), BF16), (((0,), (0,)), ((), ())), preferred_element_type=F32
        )[:, 0:1]
        lax.fori_loop(1, N_WIDE, wait_row, 0, unroll=7)
        arrived_f[...] = arrived[...].astype(F32)
        columns = jnp.concatenate([arrived_f[:, j, :] for j in range(16)], axis=1).astype(BF16)
        placed = lax.dot_general(put, columns, (((0,), (0,)), ((), ())), preferred_element_type=F32)
        hidden = jnp.where(flag > 0.5, placed, text_ref[...].astype(F32))
        scale = lax.rsqrt(jnp.mean(hidden * hidden, axis=-1, keepdims=True) + EPSILON)
        scaled = hidden * scale
        moe_in = (scaled * egain_ref[...]).astype(BF16)
        attn_in = (scaled * again_ref[...]).astype(BF16)
        for s, (start, width) in enumerate(SLICES):
            gs[s][0] = moe_in[:, start:start + width]
        for k in NEAR_FIRST:
            for s in range(3):
                hop1[s, k].start()
        loads[0].wait()
        loads[1].wait()
        own_keys = jnp.dot(attn_in, kproj[...], preferred_element_type=F32).astype(BF16)
        own_values = jnp.dot(attn_in, vproj[...], preferred_element_type=F32).astype(BF16)
        kv[narrow, :, 0:KVH * HD] = own_keys
        kv[narrow, :, KVH * HD:] = own_values
        kv_copy.start()

        half_copy.wait_send()
        for copies in (halves, spot_copies):
            for copy in copies:
                copy.wait_send()

    pl.run_scoped(
        vision,
        pltpu.VMEM((DV, FH), BF16),
        pltpu.VMEM((FH, DV), BF16),
        pltpu.VMEM((2, DV, D // 2), BF16),
        pltpu.VMEM((MERGE * TOK, DV), BF16),
        pltpu.VMEM((MERGE, TOK, DV), F32),
        pltpu.VMEM((MERGE, TOK, DV), BF16),
        pltpu.VMEM((N_WIDE, D // 2), BF16),
        pltpu.VMEM((N_WIDE, 2, 8, TOK), F32),
        pltpu.VMEM((N_WIDE, 16, TOK), BF16),
        pltpu.VMEM((N_WIDE, 16, TOK), F32),
    )

    def experts(acc0, acc1, part):
        accs = (acc0, acc1)

        def slot_blocks(p, s, kb, weighted):
            axis_a, axis_b, axis_c = ORDERS[s]
            first, count = PARTS[p]
            slot_iota = lane_iota((LINE * count, LINE * TOK), 0).astype(F32)
            blocks = []
            for kc in range(4):
                expert = wide_of(shifted(shifted(place, axis_b, kb), axis_c, kc))
                rows = []
                weights = []
                for ka in range(4):
                    slot = 0 if ka == 0 else 1 + axis_a * 3 + ka - 1
                    row = tables[slot, 0, pl.ds(expert, 1), :]
                    inside = (row >= float(first)) & (row < float(first + count))
                    rows.append(jnp.where(inside, row + float(count * ka - first), -1.0))
                    if weighted:
                        weights.append(tables[slot, 1, pl.ds(expert, 1), :])
                hit = slot_iota == jnp.concatenate(rows, axis=1)
                if weighted:
                    value = jnp.where(hit, jnp.concatenate(weights, axis=1), 0.0)
                else:
                    value = jnp.where(hit, 1.0, 0.0)
                blocks.append(value.astype(BF16))
            return jnp.concatenate(blocks, axis=0)

        for copy in table_copies:
            copy.wait_recv()

        hop2 = {}

        def build(p, kb):
            for s, (start, width) in enumerate(SLICES):
                tokens = gs[s][...].reshape(LINE * TOK, width)
                rows = jnp.dot(slot_blocks(p, s, kb, False), tokens, preferred_element_type=F32)
                rows = rows.astype(BF16).reshape(4, LINE * PARTS[p][1], width)
                if kb == 0:
                    mids[p][s][0] = rows
                else:
                    txs[p][s][kb] = rows
                    copy = remote(
                        txs[p][s].at[kb], mids[p][s].at[kb], s2send.at[p, s, kb],
                        s2recv.at[p, s, kb], peer(ORDERS[s][1], kb),
                    )
                    copy.start()
                    hop2[p, s, kb] = copy

        hop3 = {}

        def forward(p, kb):
            for s in range(3):
                if kb:
                    hop2[p, s, kb].wait_recv()
                for kc in NEAR_FIRST:
                    copy = remote(
                        mids[p][s].at[kb, kc], rxs[p][s].at[kc, kb], s3send.at[p, s, kc, kb],
                        s3recv.at[p, s, kc, kb], peer(ORDERS[s][2], kc),
                    )
                    copy.start()
                    hop3[p, s, kc, kb] = copy

        def sent(p):
            for (part_of, _, _), copy in hop2.items():
                if part_of == p:
                    copy.wait_send()

        def attend(head, group, allowed):
            columns = pl.ds(pl.multiple_of(head * HD, HD), HD)
            keys = kv[:, :, group * HD:(group + 1) * HD].reshape(2 * TOK, HD)
            values = kv[:, :, (KVH + group) * HD:(KVH + group + 1) * HD].reshape(2 * TOK, HD)
            scores = lax.dot_general(
                queries[:, columns], keys, (((1,), (1,)), ((), ())), preferred_element_type=F32
            ) * HD ** (-0.5)
            scores = jnp.where(allowed, scores, -1e30)
            row_max = jnp.max(scores, axis=-1, keepdims=True)
            weights = jnp.exp(scores - row_max)
            total = jnp.sum(weights, axis=-1, keepdims=True)
            mixed = jnp.dot(weights.astype(BF16), values, preferred_element_type=F32)
            attended_ref[:, columns] = (mixed / total).astype(BF16)

        def attend_heads(first, count, group):
            row_pos = lane_iota((TOK, 2 * TOK), 0) + narrow * TOK
            key_pos = lane_iota((TOK, 2 * TOK), 1)
            allowed = key_pos <= jnp.minimum(row_pos, length_ref[0] - 1)

            def body(i, carry):
                for j in range(4):
                    attend(first + i * 4 + j, group, allowed)
                return carry
            lax.fori_loop(0, count // 4, body, 0)

        written = set()

        def project(p, kc):
            count = PARTS[p][1]
            for s, (start, width) in enumerate(SLICES):
                if kc:
                    for kb in range(4):
                        hop3[p, s, kc, kb].wait_recv()
                    rows = rxs[p][s][kc].reshape(16 * count, width)
                else:
                    rows = mids[p][s][:, 0].reshape(16 * count, width)
                for n in range(2):
                    out = jnp.dot(
                        rows, gu[start:start + width, n * FE:(n + 1) * FE], preferred_element_type=F32
                    ).reshape(4, 4, count, FE)
                    for kb in range(4):
                        for ka in range(4):
                            index = source_index(ORDERS[s], ka, kb, kc)
                            if (p, n, index) in written:
                                accs[p][index, :, n * FE:(n + 1) * FE] += out[kb, ka]
                            else:
                                written.add((p, n, index))
                                accs[p][index, :, n * FE:(n + 1) * FE] = out[kb, ka]

        def activate(p):
            acc = accs[p]

            def body(i, carry):
                gate = acc[i, :, 0:FE]
                up = acc[i, :, FE:]
                acc[i, :, 0:FE] = gate * (1.0 / (1.0 + jnp.exp(-gate))) * up
                return carry

            lax.fori_loop(0, 64, body, 0)
            for (part_of, _, _, _), copy in hop3.items():
                if part_of == p:
                    copy.wait_send()
            for s in range(3):
                for kb in (1, 2, 3):
                    pl.semaphore_signal(
                        free_sem.at[p, s, kb], inc=1, device_id=peer(ORDERS[s][1], kb),
                        device_id_type=MESH,
                    )

        back1 = {}

        def give_back(p, kc):
            count = PARTS[p][1]
            for s, (start, width) in enumerate(SLICES):
                pieces = [
                    accs[p][source_index(ORDERS[s], ka, kb, kc), :, 0:FE]
                    for kb in range(4) for ka in range(4)
                ]
                active = jnp.concatenate(pieces, axis=0).astype(BF16)
                out = jnp.dot(active, dn[:, start:start + width], preferred_element_type=F32)
                out = out.astype(BF16).reshape(4, LINE * count, width)
                if kc == 0:
                    txs[p][s][:, 0] = out
                else:
                    rxs[p][s][kc] = out
                    for kb in (1, 3, 2, 0):
                        copy = remote(
                            rxs[p][s].at[kc, kb], txs[p][s].at[kb, kc], r1send.at[p, s, kc, kb],
                            r1recv.at[p, s, kc, kb], peer(ORDERS[s][2], -kc),
                        )
                        copy.start()
                        back1[p, s, kc, kb] = copy

        back2 = {}

        def back(p, kb):
            for s in range(3):
                for kc in NEAR_FIRST:
                    back1[p, s, kc, kb].wait_recv()
                if kb:
                    pl.semaphore_wait(free_sem.at[p, s, kb], 1)
                    copy = remote(
                        txs[p][s].at[kb], mids[p][s].at[kb], r2send.at[p, s, kb],
                        r2recv.at[p, s, kb], peer(ORDERS[s][1], -kb),
                    )
                    copy.start()
                    back2[p, s, kb] = copy

        def combine(p, kb, s):
            start, width = SLICES[s]
            if kb:
                back2[p, s, kb].wait_recv()
                rows = mids[p][s][kb].reshape(16 * PARTS[p][1], width)
            else:
                rows = txs[p][s][0].reshape(16 * PARTS[p][1], width)
            total = lax.dot_general(
                slot_blocks(p, s, kb, True), rows, (((0,), (0,)), ((), ())),
                preferred_element_type=F32,
            )
            if p or kb:
                part[:, start:start + width] += total
            else:
                part[:, start:start + width] = total

        for s in range(3):
            for k in (1, 2, 3):
                hop1[s, k].wait_recv()
        for kb in (1, 3, 2, 0):
            build(0, kb)
        forward(0, 0)
        kv_copy.wait_recv()
        loads[2].wait()
        attend_heads(0, 16, 0)
        forward(0, 1)
        forward(0, 3)
        for kb in (1, 3, 2, 0):
            build(1, kb)
        sent(0)
        forward(0, 2)
        forward(1, 0)
        attend_heads(16, 16, 1)
        for load in loads[3:]:
            load.wait()
        for copy in weight_copies:
            copy.wait_recv()
        project(0, 0)
        forward(1, 1)
        forward(1, 3)
        project(0, 1)
        project(0, 3)
        sent(1)
        forward(1, 2)
        project(0, 2)
        activate(0)
        for kc in (1, 3, 2, 0):
            give_back(0, kc)
        for kc in (0, 1, 3, 2):
            project(1, kc)
        activate(1)
        back(0, 1)
        back(0, 3)
        for kc in (1, 3, 2, 0):
            give_back(1, kc)
        back(0, 2)
        back(0, 0)
        for s in range(3):
            combine(0, 0, s)
        for kb in (1, 3, 2, 0):
            back(1, kb)
        for kb in (1, 3, 2):
            for s in range(3):
                combine(0, kb, s)

        back3 = {}
        for s, (start, width) in enumerate(SLICES):
            for kb in (0, 1, 3, 2):
                combine(1, kb, s)
            for k in (2, 1, 3):
                gs[s][k] = part[k * TOK:(k + 1) * TOK, start:start + width].astype(BF16)
                copy = remote(
                    gs[s].at[k], fins[s].at[k], r3send.at[s, k], r3recv.at[s, k],
                    peer(ORDERS[s][0], -k),
                )
                copy.start()
                back3[s, k] = copy
        for s, (start, width) in enumerate(SLICES):
            total = part[0:TOK, start:start + width]
            for k in (1, 3, 2):
                back3[s, k].wait_recv()
                total = total + fins[s][k].astype(F32)
            mix_ref[:, start:start + width] = total.astype(BF16)

        kv_copy.wait_send()
        for copies in (table_copies, weight_copies, hop1.values(), back1.values(), back2.values(),
                       back3.values()):
            for copy in copies:
                copy.wait_send()

    pl.run_scoped(
        experts,
        pltpu.VMEM((64, PARTS[0][1], 2 * FE), F32),
        pltpu.VMEM((64, PARTS[1][1], 2 * FE), F32),
        pltpu.VMEM((LINE * TOK, D), F32),
    )


def layer(
    patches, gain, spots, text, again, egain, routes, rweight, lengths, vup, vdown, merger,
    queries, kproj, vproj, gate, up, down,
):
    vmem = pl.BlockSpec(memory_space=pltpu.VMEM)
    smem = pl.BlockSpec(memory_space=pltpu.SMEM)
    hbm = pl.BlockSpec(memory_space=pl.ANY)
    dma = pltpu.SemaphoreType.DMA
    widths = [width for _, width in SLICES]
    scratch = [
        pltpu.VMEM((D, 2 * FE), BF16),
        pltpu.VMEM((FE, D), BF16),
        pltpu.VMEM((TOK, HQ * HD), BF16),
        pltpu.VMEM((D, KVH * HD), BF16),
        pltpu.VMEM((D, KVH * HD), BF16),
        pltpu.VMEM((2, TOK, 2 * KVH * HD), BF16),
        pltpu.VMEM((10, 2, 64, TOK), F32),
        pltpu.VMEM((MERGE, TOK, DV), BF16),
        pltpu.VMEM((N_WIDE, D // 2), BF16),
        pltpu.VMEM((N_WIDE, 16, TOK), BF16),
        pltpu.VMEM((4, 4, 4, 8, TOK), F32),
    ]
    scratch += [pltpu.VMEM((4, TOK, w), BF16) for w in widths]
    scratch += [pltpu.VMEM((4, TOK, w), BF16) for w in widths]
    for _ in range(3):
        for _, count in PARTS:
            scratch += [pltpu.VMEM((4, 4, LINE * count, w), BF16) for w in widths]
    scratch += [
        dma((12,)), dma((3,)), dma((3,)), dma, dma, dma((10,)), dma((10,)),
        dma((3, 4)), dma((3, 4)), dma((2, 3, 4)), dma((2, 3, 4)),
        dma((2, 3, 4, 4)), dma((2, 3, 4, 4)), dma((2, 3, 4, 4)), dma((2, 3, 4, 4)),
        dma((2, 3, 4)), dma((2, 3, 4)), dma((3, 4)), dma((3, 4)),
        pltpu.SemaphoreType.REGULAR((2, 3, 4)),
        dma((4,)), dma((4,)), dma, dma, dma((3, 4)), dma((3, 4)),
        dma((N_WIDE,)), dma((N_WIDE,)),
    ]
    return pl.pallas_call(
        layer_kernel,
        out_shape=(
            jax.ShapeDtypeStruct((TOK, HQ * HD), BF16),
            jax.ShapeDtypeStruct((TOK, D), BF16),
        ),
        in_specs=[vmem] * 8 + [smem] + [hbm] * 9,
        out_specs=(vmem, vmem),
        scratch_shapes=scratch,
        compiler_params=pltpu.CompilerParams(
            collective_id=0, has_side_effects=True, vmem_limit_bytes=64 << 20
        ),
        name="layer",
    )(
        patches, gain, spots, text, again, egain, routes, rweight, lengths, vup, vdown, merger,
        queries, kproj, vproj, gate, up, down,
    )


def local(
    patches,
    vision_gain,
    vision_up,
    vision_down,
    merger,
    visual_spots,
    text_embed,
    queries,
    attention_gain,
    key_proj,
    value_proj,
    prompt_lengths,
    expert_gain,
    routes,
    route_weight,
    gate_weight,
    up_weight,
    down_weight,
):
    return layer(
        patches, vision_gain, visual_spots.reshape(1, -1), text_embed,
        attention_gain.reshape(1, -1), expert_gain.reshape(1, -1), routes.T, route_weight.T,
        prompt_lengths, vision_up, vision_down, merger, queries, key_proj, value_proj, gate_weight,
        up_weight, down_weight,
    )


def solution(mesh):
    return jax.shard_map(
        local,
        mesh=mesh,
        in_specs=(
            P("wide", None),
            P(),
            P(None, "narrow"),
            P("narrow", None),
            P(None, "narrow"),
            P("wide"),
            P(("wide", "narrow"), None),
            P(("wide", "narrow"), None),
            P(),
            P(),
            P(),
            P("wide"),
            P(),
            P(("wide", "narrow"), None),
            P(("wide", "narrow"), None),
            P("wide", None, "narrow"),
            P("wide", None, "narrow"),
            P("wide", "narrow", None),
        ),
        out_specs=(P(("wide", "narrow"), None), P(("wide", "narrow"), None)),
        check_vma=False,
    )
```
